32 devices in a mesh: dp: 4 (over y, x), ep: 8 (over z, core).
Axes of the slice: x: 2, y: 2, z: 4, core: 2. Of those that a mesh axis runs over, the one named last changes fastest.
Arguments:
- tokens: bfloat16 [24576, 1024], P(('dp', 'ep')), may hold values from -6 to 6
- lengths: int32 [32], P(('dp', 'ep')), may hold values from 256 to 768, as said below
- key_mask: int32 [24576], P(('dp', 'ep')), may hold values 0 or 1
- routes: int32 [24576, 1], P(('dp', 'ep')), may hold values from 0 to 7; in each aligned block of 768 rows (0 to 767, 768 to 1535, ...) at most 120 rows name the same one
- norm1_gain: float32 [1024], replicated, may hold values from 0.5 to 1.5
- norm1_bias: float32 [1024], replicated, may hold values from -2.5 to 2.5
- qkv_weight: bfloat16 [1024, 3072], replicated, may hold values from -0.1875 to 0.1875
- out_weight: bfloat16 [1024, 1024], replicated, may hold values from -1.5 to 1.5
- norm2_gain: float32 [1024], replicated, may hold values from 0.5 to 1.5
- norm2_bias: float32 [1024], replicated, may hold values from -2.5 to 2.5
- up_weight: bfloat16 [1024, 4096], replicated, may hold values from -0.1875 to 0.1875
- down_weight: bfloat16 [4096, 1024], replicated, may hold values from -0.09375 to 0.09375
- router_weight: bfloat16 [1024, 8], replicated, may hold values from -0.125 to 0.125
- mix_weight: bfloat16 [1024, 2], replicated, may hold values from -0.125 to 0.125
- expert_up: bfloat16 [8, 1024, 4096], P('ep'), may hold values from -0.1875 to 0.1875
- expert_down: bfloat16 [8, 4096, 1024], P('ep'), may hold values from -0.75 to 0.75
- cotangent: bfloat16 [24576, 1024], P(('dp', 'ep')), may hold values from -6 to 6
Outputs:
- outputs: bfloat16 [24576, 1024], P(('dp', 'ep'))
- grad_inputs: bfloat16 [24576, 1024], P(('dp', 'ep'))
- grad_norm1_gain: float32 [1024], P(('dp', 'ep'))
- grad_norm1_bias: float32 [1024], P(('dp', 'ep'))
- grad_qkv_weight: float32 [1024, 3072], P(None, ('dp', 'ep'))
- grad_out_weight: float32 [1024, 1024], P(('dp', 'ep'))
- grad_norm2_gain: float32 [1024], P(('dp', 'ep'))
- grad_norm2_bias: float32 [1024], P(('dp', 'ep'))
- grad_up_weight: float32 [1024, 4096], P('ep', 'dp')
- grad_down_weight: float32 [4096, 1024], P('dp', 'ep')
- grad_router_weight: float32 [1024, 8], P(('dp', 'ep'))
- grad_mix_weight: float32 [1024, 2], P(('dp', 'ep'))
- grad_expert_up: float32 [8, 1024, 4096], P('ep', None, 'dp')
- grad_expert_down: float32 [8, 4096, 1024], P('ep', 'dp')
The draws below stay inside these ranges and needn't reach their ends.
Inputs may be any that keep to these rules, and one draw needn't show every extreme that they name: `lengths`: each slot holds one sequence of that many tokens from its start; the rest of the slot is padding. `routes`: among the rows of one device, at most 120 name the same expert.
All inputs are finite; a program needn't handle non-finite values. No bound on the sum of `key_mask` on one device may be relied on, other than what follows from the above.
Results may differ from the reference program's by a relative error of at most 0.015.
Values may be sent and summed in bfloat16 or wider, within the bound.
No kernel may reach another device: no remote copies, remote signals or barrier semaphores. Data moves between devices by JAX's collectives and lax.ppermute only.
A program may use at most 384 MiB of HBM per device.

```python
import math
import jax
import jax.numpy as jnp
import numpy as np
from jax import lax

D = 1024
HEADS = 16
HEAD_DIM = 64
FF = 4096
SLOT = 768
MIN_LEN = 256
SEQ_DEV = 1
EXPERTS = 8
CAP = 120
SEQS = 32
TOKENS = 24576
N_DP = 4
N_EP = 8


def draw_lengths(key, part):
    key = jax.random.fold_in(key, 7)
    base_key, first_key, second_key = jax.random.split(key, 3)
    drawn = jax.random.randint(base_key, (SEQS,), MIN_LEN, SLOT + 1)
    longest = jax.random.randint(first_key, (), 0, SEQS)
    offset = jax.random.randint(second_key, (), 1, SEQS)
    shortest = (longest + offset) % SEQS
    drawn = drawn.at[longest].set(SLOT)
    drawn = drawn.at[shortest].set(MIN_LEN)
    return drawn.astype(jnp.int32)


def place_ends(entries, rng, low, top_value):
    dims = entries.shape
    index_at = [jax.random.randint(jax.random.fold_in(rng, axis), (), 0, dims[axis]) for axis in range(len(dims))]
    entries = entries.at[tuple(index_at)].set(low)
    longest = dims.index(max(dims))
    index_at[longest] = (index_at[longest] + 1) % dims[longest]
    return entries.at[tuple(index_at)].set(top_value)


def steps_of(rng, extent, shards, least, top_value):
    factor_of = 1.0
    for dim, parts in shards:
        heights = jax.random.uniform(jax.random.fold_in(jax.random.fold_in(rng, 6), dim), (parts,), jnp.float32, least / len(shards), top_value / len(shards))
        factor_of = factor_of * jnp.repeat(jnp.exp(heights), extent[dim] // parts).reshape((-1,) + (1,) * (len(extent) - 1 - dim))
    return factor_of


def routed_block(own_key, own, number, rows, number_of, top, reach, skew):
    ranking = jax.random.permutation(own_key, number_of)
    heavy_load, common = shares(number_of, rows * top, reach, skew, True), shares(number_of, rows * top, reach, skew, False)
    places = jnp.arange(number_of)

    def named(sizes, rotation):
        used = int((sizes > 0).sum())
        fixed = max(1, used // 4)
        moved = fixed + (places - fixed + rotation * (used - fixed)) % max(1, number_of - fixed)
        return jnp.zeros((number_of,), jnp.int32).at[ranking[jnp.where(places < fixed, places, moved)]].set(jnp.asarray(sizes, jnp.int32))

    sizes = jnp.where(number % 4 == 0, named(heavy_load, number // 4), named(common, number - number // 4 - 1))
    mixed = jax.random.permutation(jax.random.fold_in(own, 3), number_of)
    source_of, sink = mixed[0:number_of // 2 * 2:2], mixed[1:number_of // 2 * 2:2]
    margin = jnp.minimum(sizes[source_of] - 1, reach - sizes[sink]) // 2
    margin = jnp.where((source_of == ranking[0]) | (sink == ranking[0]) | (sizes[sink] == 0), 0, jnp.maximum(margin, 0))
    moved = jax.random.randint(jax.random.fold_in(own, 4), (number_of // 2,), 0, 1 << 20) % (margin + 1)
    sizes = sizes.at[source_of].add(-moved).at[sink].add(moved)
    members = jnp.searchsorted(jnp.cumsum(sizes), jnp.arange(rows * top), side="right").astype(jnp.int32)
    listing = members.reshape(top, rows).T
    listing = listing[jax.random.permutation(jax.random.fold_in(own, 1), rows)]
    rotation = jax.random.randint(jax.random.fold_in(own, 2), (rows, 1), 0, top)
    return jnp.take_along_axis(listing, (jnp.arange(top)[None, :] + rotation) % top, axis=1)


def shares(number_of, total, limit, skew, full):
    portions = [(1 << 20) // math.isqrt(rank ** skew) + 1 for rank in range(1, number_of + 1)]
    largest = limit if full else min(limit, max(-(-total // number_of), total * portions[0] // sum(portions)))
    least = 1 if total - largest >= number_of - 1 else 0
    holding, spare = [largest] + [least] * (number_of - 1), total - largest - least * (number_of - 1)
    while spare > 0:
        movable = [i for i in range(1, number_of) if holding[i] < largest] or [i for i in range(1, number_of) if holding[i] < limit]
        mass, budget = sum([portions[i] for i in movable]), spare
        for i in movable:
            more = min(limit - holding[i], max(1, budget * portions[i] // mass), spare)
            holding[i] = holding[i] + more
            spare = spare - more
    return np.array(holding)


def bell_draw(own_key, shape, scale, limit, cuts=(), kind=jnp.bfloat16):
    entries = scale * jax.random.normal(own_key, shape, jnp.float32)
    if cuts:
        entries = entries * steps_of(own_key, shape, cuts, -0.22, 0.18)
    return jnp.clip(entries, -limit, limit).astype(kind)


def setup_inputs(seed: int = 0) -> dict:
    arg_keys = jax.random.split(jax.random.key(seed), 18)
    tokens = bell_draw(arg_keys[0], (TOKENS, D), 1.0, 6.0, ((0, 32),))
    lengths = draw_lengths(jax.random.fold_in(arg_keys[17], 71), 0)
    key_mask = place_ends((jax.random.randint(arg_keys[2], (TOKENS,), 0, 8) < 7).astype(jnp.int32), jax.random.fold_in(arg_keys[2], 1), 0, 1)
    routes_keys = jax.random.split(jax.random.fold_in(arg_keys[3], 1), TOKENS // (SLOT * SEQ_DEV))
    routes_turns = jax.random.permutation(jax.random.fold_in(arg_keys[3], 3), TOKENS // (SLOT * SEQ_DEV))
    routes = jax.vmap(lambda own, number: routed_block(jax.random.fold_in(arg_keys[3], 2), own, number, SLOT * SEQ_DEV, EXPERTS, 1, CAP, 1))(routes_keys, routes_turns).reshape((TOKENS, 1))
    norm1_gain = jnp.clip(1.0 + 0.1 * jax.random.normal(arg_keys[4], (D,), jnp.float32), 0.5, 1.5)
    norm1_bias = bell_draw(arg_keys[5], (D,), 0.3, 2.5, (), jnp.float32)
    qkv_weight = bell_draw(arg_keys[6], (D, 3 * D), D ** -0.5, 0.1875)
    out_weight = bell_draw(arg_keys[7], (D, D), (D // 64) ** -0.5, 1.5)
    norm2_gain = jnp.clip(1.0 + 0.1 * jax.random.normal(arg_keys[8], (D,), jnp.float32), 0.5, 1.5)
    norm2_bias = bell_draw(arg_keys[9], (D,), 0.3, 2.5, (), jnp.float32)
    up_weight = bell_draw(arg_keys[10], (D, FF), D ** -0.5, 0.1875)
    down_weight = bell_draw(arg_keys[11], (FF, D), FF ** -0.5, 0.09375)
    router_weight = bell_draw(arg_keys[12], (D, EXPERTS), (2 * D) ** -0.5, 0.125)
    mix_weight = bell_draw(arg_keys[13], (D, 2), (2 * D) ** -0.5, 0.125)
    expert_up = bell_draw(arg_keys[14], (EXPERTS, D, FF), D ** -0.5, 0.1875, ((0, 8),))
    expert_down = bell_draw(arg_keys[15], (EXPERTS, FF, D), (max(1, FF // (EXPERTS * EXPERTS))) ** -0.5, 0.75, ((0, 8),))
    cotangent = bell_draw(arg_keys[16], (TOKENS, D), 1.0, 6.0, ((0, 32),))
    return {"tokens": tokens, "lengths": lengths, "key_mask": key_mask, "routes": routes, "norm1_gain": norm1_gain, "norm1_bias": norm1_bias, "qkv_weight": qkv_weight, "out_weight": out_weight, "norm2_gain": norm2_gain, "norm2_bias": norm2_bias, "up_weight": up_weight, "down_weight": down_weight, "router_weight": router_weight, "mix_weight": mix_weight, "expert_up": expert_up, "expert_down": expert_down, "cotangent": cotangent}


@jax.custom_vjp
def low(v):
    return lax.optimization_barrier(v.astype(jnp.bfloat16)).astype(jnp.float32)

@jax.custom_vjp
def low_back(v):
    return v

def low_keep(v):
    return (low(v), None)

def low_pass(kept, grad):
    return (grad,)

def back_keep(v):
    return (v, None)

def back_low(kept, grad):
    return (low(grad),)
low.defvjp(low_keep, low_pass)
low_back.defvjp(back_keep, back_low)
epsilon = 1e-05
precise = lax.Precision.HIGHEST
masked_score = -1e+30

def layer_norm(values, norm_gain, norm_bias):
    average = lax.optimization_barrier(jnp.mean(values, axis=-1, keepdims=True))
    centered = values - average
    variance = lax.optimization_barrier(jnp.mean(centered * centered, axis=-1, keepdims=True))
    return centered * lax.rsqrt(variance + epsilon) * norm_gain + norm_bias

def smooth_gate(values):
    return jax.nn.gelu(values, approximate=True)

def softmax_rows(values):
    row_top = lax.optimization_barrier(jnp.max(values, axis=-1, keepdims=True))
    raised = jnp.exp(values - row_top)
    return raised / lax.optimization_barrier(jnp.sum(raised, axis=-1, keepdims=True))

def allowed_keys(length, mask_slot):
    row_count = mask_slot.shape[0]
    position = jnp.arange(row_count)
    earlier = position[None, :] <= position[:, None]
    usable = (position < length) & (mask_slot == 1)
    itself = position[None, :] == position[:, None]
    return earlier & (usable[None, :] | itself)

def split_heads(qkv_slot):
    row_count = qkv_slot.shape[0]
    queries = qkv_slot[:, :D].reshape(row_count, HEADS, HEAD_DIM)
    key_rows = qkv_slot[:, D:2 * D].reshape(row_count, HEADS, HEAD_DIM)
    value_rows = qkv_slot[:, 2 * D:].reshape(row_count, HEADS, HEAD_DIM)
    return (queries, key_rows, value_rows)

def attend(packed):
    qkv_slot, length, mask_slot = packed
    queries, key_rows, value_rows = split_heads(qkv_slot)
    scores = low_back(jnp.einsum('qhd,khd->hqk', queries, key_rows, precision=precise) * HEAD_DIM ** (-0.5))
    masked = jnp.where(allowed_keys(length, mask_slot)[None], scores, masked_score)
    weights = low(softmax_rows(masked))
    context = jnp.einsum('hqk,khd->qhd', weights, value_rows, precision=precise)
    return context.reshape(qkv_slot.shape[0], D)

def reference(tokens, lengths, key_mask, routes, norm1_gain, norm1_bias, qkv_weight, out_weight, norm2_gain, norm2_bias, up_weight, down_weight, router_weight, mix_weight, expert_up, expert_down, cotangent):
    row_live = jnp.arange(TOKENS) % SLOT < jnp.repeat(lengths, SLOT, total_repeat_length=TOKENS)
    live_scale = row_live.astype(jnp.float32)
    flat_routes = routes[:, 0]
    onehot = (flat_routes[:, None] == jnp.arange(EXPERTS)[None, :]).astype(jnp.float32)
    per_expert = N_DP * N_EP * CAP
    mask_slots = key_mask.reshape(SEQS, SLOT)

    def find_rows(expert):
        picked = (flat_routes == expert) & row_live
        found_rows = jnp.nonzero(picked, size=per_expert, fill_value=0)[0].astype(jnp.int32)
        valid_slots = (jnp.arange(per_expert) < jnp.sum(picked.astype(jnp.int32))).astype(jnp.float32)
        return (found_rows, valid_slots)
    expert_index, expert_valid = lax.map(find_rows, jnp.arange(EXPERTS))

    def forward(inputs, first_gain, first_bias, qkv_float, out_float, second_gain, second_bias, up_float, down_float, router_float, mix_float, expert_up_float, expert_down_float):
        first = low(layer_norm(inputs, first_gain, first_bias))
        qkv = low(low_back(jnp.dot(first, qkv_float, precision=precise)))
        context = lax.map(jax.checkpoint(attend), (qkv.reshape(SEQS, SLOT, 3 * D), lengths, mask_slots))
        context = low(low_back(context.reshape(TOKENS, D)))
        attended = low_back(jnp.dot(context, out_float, precision=precise))
        middle = inputs + attended
        second = low(layer_norm(middle, second_gain, second_bias))
        dense_pre = low_back(jnp.dot(second, up_float, precision=precise))
        dense_out = low_back(jnp.dot(low(smooth_gate(dense_pre)), down_float, precision=precise))
        router_probs = softmax_rows(jnp.dot(second, router_float, precision=precise))
        chosen = lax.optimization_barrier(jnp.sum(router_probs * onehot, axis=1)) * live_scale
        mixing = softmax_rows(jnp.dot(second, mix_float, precision=precise))

        def one_expert(packed):
            up_one, down_one, row_index, valid_slots = packed
            arriving = low_back(second[row_index])
            expert_pre = low_back(jnp.dot(arriving, up_one, precision=precise))
            expert_hidden = low(smooth_gate(expert_pre))
            expert_out = low(low_back(jnp.dot(expert_hidden, down_one, precision=precise)))
            return expert_out * valid_slots[:, None]
        expert_outs = lax.map(jax.checkpoint(one_expert), (expert_up_float, expert_down_float, expert_index, expert_valid))
        expert_rows = jnp.zeros((TOKENS, D), jnp.float32).at[expert_index.reshape(-1)].add(expert_outs.reshape(-1, D))
        return middle + mixing[:, 0:1] * dense_out + mixing[:, 1:2] * (chosen[:, None] * expert_rows)
    floats = (tokens.astype(jnp.float32), norm1_gain.astype(jnp.float32), norm1_bias.astype(jnp.float32), qkv_weight.astype(jnp.float32), out_weight.astype(jnp.float32), norm2_gain.astype(jnp.float32), norm2_bias.astype(jnp.float32), up_weight.astype(jnp.float32), down_weight.astype(jnp.float32), router_weight.astype(jnp.float32), mix_weight.astype(jnp.float32), expert_up.astype(jnp.float32), expert_down.astype(jnp.float32))
    outputs, pullback = jax.vjp(forward, *floats)
    grads = pullback(cotangent.astype(jnp.float32))
    return (outputs.astype(jnp.bfloat16), grads[0].astype(jnp.bfloat16), grads[1], grads[2], grads[3], grads[4], grads[5], grads[6], grads[7], grads[8], grads[9], grads[10], grads[11], grads[12])
```

```python
import functools

import jax
import jax.numpy as jnp
from jax import lax
from jax.experimental import pallas as pl
from jax.experimental.pallas import tpu as pltpu
from jax.sharding import PartitionSpec as P

HEAD_DIM = 64
EPSILON = 1e-05
MASKED = -1e30
ROW_BLOCK = 256
CHUNKS = 2
LANES = 128
GELU_ROOT = 0.7978845608028654
GELU_CUBE = 0.044715

f32 = jnp.float32
bf16 = jnp.bfloat16


def dot_nn(a, b):
    return lax.dot_general(a, b, (((1,), (0,)), ((), ())), preferred_element_type=f32)


def dot_nt(a, b):
    return lax.dot_general(a, b, (((1,), (1,)), ((), ())), preferred_element_type=f32)


def call(kernel, grid, in_specs, out_specs, out_shape, flops, scratch=(), prefetch=0, name=None):
    spec = pltpu.PrefetchScalarGridSpec(
        num_scalar_prefetch=prefetch,
        grid=grid,
        in_specs=in_specs,
        out_specs=out_specs,
        scratch_shapes=list(scratch),
    )
    return pl.pallas_call(
        kernel,
        grid_spec=spec,
        out_shape=out_shape,
        compiler_params=pltpu.CompilerParams(
            dimension_semantics=("arbitrary",) * len(grid), vmem_limit_bytes=56 * 1024 * 1024
        ),
        cost_estimate=pl.CostEstimate(
            flops=int(flops), bytes_accessed=int(flops / 400), transcendentals=0
        ),
        name=name,
    )


def fixed(shape):
    return pl.BlockSpec(
        shape, lambda *_: (0,) * len(shape), pipeline_mode=pl.Buffered(buffer_count=1)
    )


def kept(shape):
    return pl.BlockSpec(shape, lambda *_: (0,) * len(shape))


def rows_of(height, width):
    return pl.BlockSpec((height, width), lambda i, *_: (i, 0))


def shape_of(shape, dtype):
    return jax.ShapeDtypeStruct(shape, dtype)


def normalized(values):
    average = jnp.mean(values, axis=1, keepdims=True)
    centered = values - average
    root = lax.rsqrt(jnp.mean(centered * centered, axis=1, keepdims=True) + EPSILON)
    return centered * root, root


def gelu_pair(v):
    square = v * v
    t = jnp.tanh(v * (GELU_ROOT + (GELU_ROOT * GELU_CUBE) * square))
    half = 0.5 + 0.5 * t
    slope = half + (v * (0.5 - 0.5 * (t * t))) * (
        GELU_ROOT + (3.0 * GELU_ROOT * GELU_CUBE) * square
    )
    return v * half, slope


def ln_qkv_kernel(x_ref, g_ref, b_ref, w_ref, first_ref, qkv_ref):
    @pl.when(pl.program_id(0) == 0)
    def _():
        def some_rows(i, carry):
            at = pl.ds(pl.multiple_of(i * LANES, LANES), LANES)
            n, _ = normalized(x_ref[at, :].astype(f32))
            first_ref[at, :] = (n * g_ref[...] + b_ref[...]).astype(bf16)
            return carry

        lax.fori_loop(0, x_ref.shape[0] // LANES, some_rows, 0)

    qkv_ref[...] = dot_nn(first_ref[...], w_ref[...]).astype(bf16)


def ln_qkv(tokens, gain, bias, weight):
    rows, d = tokens.shape
    width = weight.shape[1]
    block = 512
    return call(
        ln_qkv_kernel,
        (width // block,),
        [
            fixed((rows, d)),
            fixed((1, d)),
            fixed((1, d)),
            pl.BlockSpec((d, block), lambda i: (0, i)),
        ],
        [kept((rows, d)), pl.BlockSpec((rows, block), lambda i: (0, i))],
        [shape_of((rows, d), bf16), shape_of((rows, width), bf16)],
        2 * rows * d * width,
        name="ln_qkv",
    )(tokens, gain, bias, weight)


def diagonal_bias(bias_rows):
    size = bias_rows.shape[0]
    key_at = lax.broadcasted_iota(jnp.int32, (size, size), 0)
    query_at = lax.broadcasted_iota(jnp.int32, (size, size), 1)
    return jnp.where(
        key_at == query_at, 0.0, jnp.where(key_at < query_at, bias_rows, MASKED)
    )


def head_lanes(values, head):
    lane = lax.broadcasted_iota(jnp.int32, values.shape, 1)
    inside = (lane >= head * HEAD_DIM) & (lane < (head + 1) * HEAD_DIM)
    return jnp.where(inside, values, jnp.zeros_like(values))


def attend_kernel(bias_ref, q_ref, k_ref, v_ref, ctx_ref, ctx_t_ref, lse_ref):
    rows = q_ref.shape[0]
    v_t = v_ref[...].T
    for i in range(rows // ROW_BLOCK):
        low, high = i * ROW_BLOCK, (i + 1) * ROW_BLOCK
        edge = diagonal_bias(bias_ref[low:high, :])
        q = q_ref[low:high, :] * jnp.asarray(HEAD_DIM**-0.5, bf16)
        sides = []
        for head in range(2):
            q_head = head_lanes(q, head)
            inner = dot_nt(k_ref[low:high, :], q_head) + edge
            top = jnp.max(inner, axis=0, keepdims=True)
            if i:
                outer = dot_nt(k_ref[:low, :], q_head) + bias_ref[:low, :]
                top = jnp.maximum(top, jnp.max(outer, axis=0, keepdims=True))
            inner = jnp.exp(inner - top)
            total = jnp.sum(inner, axis=0, keepdims=True)
            v_head = v_t[head * HEAD_DIM : (head + 1) * HEAD_DIM, :]
            side = dot_nn(v_head[:, low:high], inner.astype(bf16))
            if i:
                outer = jnp.exp(outer - top)
                total = total + jnp.sum(outer, axis=0, keepdims=True)
                side = side + dot_nn(v_head[:, :low], outer.astype(bf16))
            sides.append(side / total)
            lse_ref[0, head : head + 1, low:high] = top + jnp.log(total)
        both = jnp.concatenate(sides, axis=0)
        ctx_t_ref[:, low:high] = both.astype(bf16)
        ctx_ref[low:high, :] = both.T.astype(bf16)


def attend(qkv, bias):
    rows, d = qkv.shape[0], qkv.shape[1] // 3
    pairs = d // LANES

    def third(n):
        return pl.BlockSpec((rows, LANES), lambda h: (0, n * pairs + h))

    return call(
        attend_kernel,
        (pairs,),
        [fixed((rows, 1)), third(0), third(1), third(2)],
        [
            third(0),
            pl.BlockSpec((LANES, rows), lambda h: (h, 0)),
            pl.BlockSpec((1, 8, rows), lambda h: (h, 0, 0)),
        ],
        [
            shape_of((rows, d), bf16),
            shape_of((d, rows), bf16),
            shape_of((pairs, 8, rows), f32),
        ],
        8 * rows * rows * d,
        name="attend",
    )(bias, qkv, qkv, qkv)


def attend_back_kernel(
    bias_ref, lse_ref, q_ref, k_ref, v_ref, do_ref, g_ref, g_t_ref, gk_acc, gv_acc
):
    rows = q_ref.shape[0]
    scale = HEAD_DIM**-0.5
    k_t = k_ref[...].T
    gk_acc[...] = jnp.zeros_like(gk_acc)
    gv_acc[...] = jnp.zeros_like(gv_acc)
    for i in range(rows // ROW_BLOCK):
        low, high = i * ROW_BLOCK, (i + 1) * ROW_BLOCK
        edge = diagonal_bias(bias_ref[low:high, :])
        q = q_ref[low:high, :] * jnp.asarray(scale, bf16)
        do = do_ref[low:high, :]
        sides = []
        for head in range(2):
            q_head = head_lanes(q, head)
            do_head = head_lanes(do, head)
            lse = lse_ref[0, head : head + 1, low:high]
            spans = [(low, high, edge)]
            if i:
                spans.append((0, low, bias_ref[:low, :]))
            probs, grads = [], []
            dots = 0.0
            for start, stop, bias in spans:
                p = jnp.exp(dot_nt(k_ref[start:stop, :], q_head) + bias - lse)
                gp = dot_nt(v_ref[start:stop, :], do_head)
                dots = dots + jnp.sum(p * gp, axis=0, keepdims=True)
                probs.append(p)
                grads.append(gp)
            side = 0.0
            k_head = k_t[head * HEAD_DIM : (head + 1) * HEAD_DIM, :]
            for (start, stop, _), p, gp in zip(spans, probs, grads):
                ds = (p * (gp - dots)).astype(bf16)
                gv_acc[start:stop, :] += dot_nn(p.astype(bf16), do_head)
                gk_acc[start:stop, :] += dot_nn(ds, q_head)
                side = side + dot_nn(k_head[:, start:stop], ds)
            sides.append(side * scale)
        both = jnp.concatenate(sides, axis=0)
        g_t_ref[0, :, low:high] = both.astype(bf16)
        g_ref[0, low:high, :] = both.T.astype(bf16)
    for n, acc in ((1, gk_acc), (2, gv_acc)):
        g_ref[n] = acc[...].astype(bf16)
        g_t_ref[n] = acc[...].T.astype(bf16)


def attend_back(qkv, bias, lse, grad_context):
    rows, d = grad_context.shape
    pairs = d // LANES

    def third(n):
        return pl.BlockSpec((rows, LANES), lambda h: (0, n * pairs + h))

    return call(
        attend_back_kernel,
        (pairs,),
        [
            fixed((rows, 1)),
            pl.BlockSpec((1, 8, rows), lambda h: (h, 0, 0)),
            third(0),
            third(1),
            third(2),
            third(0),
        ],
        [
            pl.BlockSpec((3, rows, LANES), lambda h: (0, 0, h)),
            pl.BlockSpec((3, LANES, rows), lambda h: (0, h, 0)),
        ],
        [shape_of((3, rows, d), bf16), shape_of((3, d, rows), bf16)],
        20 * rows * rows * d,
        scratch=[pltpu.VMEM((rows, LANES), f32), pltpu.VMEM((rows, LANES), f32)],
        name="attend_back",
    )(bias, lse, qkv, qkv, qkv, grad_context)


def after_kernel(
    rb, core_ref, x_ref, ctx_ref, cot_ref, w_ref, g_ref, b_ref, mix_ref,
    middle_ref, second_ref, second_t_ref, gdl_ref, gdl_t_ref, mixing_ref,
):
    d = x_ref.shape[1]
    middle = x_ref[...].astype(f32) + dot_nn(ctx_ref[...], w_ref[...])
    middle_ref[...] = middle
    n, _ = normalized(middle)
    second = (n * g_ref[...] + b_ref[...]).astype(bf16)
    second_ref[...] = second
    logits = dot_nn(second, mix_ref[...])
    gap = logits[:, 1:2] - logits[:, 0:1]
    first_share = 1.0 / (1.0 + jnp.exp(gap))
    other_share = 1.0 / (1.0 + jnp.exp(-gap))
    lane = lax.broadcasted_iota(jnp.int32, mixing_ref.shape, 1)
    mixing_ref[...] = jnp.where(lane == 0, first_share, other_share)
    gdl = (first_share * cot_ref[...].astype(f32)).astype(bf16)
    gdl_ref[...] = gdl
    core = core_ref[0]
    for values, target in ((second, second_t_ref), (gdl, gdl_t_ref)):
        turned = values.astype(f32).T.astype(bf16)
        for piece in range(d // rb):
            place = ((piece % 2) ^ core) * (d // (2 * rb)) + piece // 2
            target[pl.ds(pl.multiple_of(place * rb, rb), rb), :] = turned[
                piece * rb : (piece + 1) * rb, :
            ]


def after(core, tokens, context, cotangent, weight, gain, bias, mix_padded, rb):
    rows, d = tokens.shape
    block = rows_of(ROW_BLOCK, d)
    turned = pl.BlockSpec((d, ROW_BLOCK), lambda i, *_: (0, i))
    return call(
        functools.partial(after_kernel, rb),
        (rows // ROW_BLOCK,),
        [block, block, block, fixed((d, d)), fixed((1, d)), fixed((1, d)), fixed((d, LANES))],
        [block, block, turned, block, turned, rows_of(ROW_BLOCK, LANES)],
        [
            shape_of((rows, d), f32),
            shape_of((rows, d), bf16),
            shape_of((d, rows), bf16),
            shape_of((rows, d), bf16),
            shape_of((d, rows), bf16),
            shape_of((rows, LANES), f32),
        ],
        2 * rows * d * d,
        prefetch=1,
        name="after",
    )(core, tokens, context, cotangent, weight, gain, bias, mix_padded)


def dense_kernel(
    owner_ref, place_ref, second_ref, second_t_ref, gdl_ref, gdl_t_ref, up_ref, down_ref,
    out_ref, gsec_ref, up_keep_ref, up_send_ref, down_keep_ref, down_send_ref, hidden, gpre,
):
    rows = second_ref.shape[0]
    half = second_t_ref.shape[0] // 2

    @pl.when(pl.program_id(0) == 0)
    def _():
        out_ref[...] = jnp.zeros_like(out_ref)
        gsec_ref[...] = jnp.zeros_like(gsec_ref)

    for low in range(0, rows, ROW_BLOCK):
        at = slice(low, low + ROW_BLOCK)
        value, slope = gelu_pair(dot_nn(second_ref[at, :], up_ref[...]))
        h = value.astype(bf16)
        g = (dot_nt(gdl_ref[at, :], down_ref[...]) * slope).astype(bf16)
        hidden[at, :] = h
        gpre[at, :] = g
        out_ref[at, :] += dot_nn(h, down_ref[...])
        gsec_ref[at, :] += dot_nt(g, up_ref[...])
    up_keep_ref[0] = dot_nn(second_t_ref[:half, :], gpre[...]).astype(bf16)
    up_send_ref[0] = dot_nn(second_t_ref[half:, :], gpre[...]).astype(bf16)
    down_keep_ref[0] = dot_nn(gdl_t_ref[:half, :], hidden[...]).astype(bf16)
    down_send_ref[0] = dot_nn(gdl_t_ref[half:, :], hidden[...]).astype(bf16)


def dense(chunk, owners, places, second, second_t, gdl, gdl_t, up, down):
    rows, d = second.shape
    n = owners.shape[0]
    width = up.shape[1] // (n * CHUNKS)

    def piece(ordered):
        def at(t, owner, place):
            return (place[t] if ordered else t, 0, 0)

        return pl.BlockSpec((1, d // 2, width), at)

    return call(
        dense_kernel,
        (n,),
        [
            fixed((rows, d)),
            fixed((d, rows)),
            fixed((rows, d)),
            fixed((d, rows)),
            pl.BlockSpec((d, width), lambda t, owner, place: (0, owner[t] * CHUNKS + chunk)),
            pl.BlockSpec((width, d), lambda t, owner, place: (owner[t] * CHUNKS + chunk, 0)),
        ],
        [kept((rows, d)), kept((rows, d)), piece(False), piece(False), piece(True), piece(True)],
        [shape_of((rows, d), f32)] * 2 + [shape_of((n, d // 2, width), bf16)] * 4,
        12 * rows * d * n * width,
        scratch=[pltpu.VMEM((rows, width), bf16), pltpu.VMEM((rows, width), bf16)],
        prefetch=2,
        name="dense",
    )(owners, places, second, second_t, gdl, gdl_t, up, down)


def expert_kernel(
    experts, me_ref, arr_ref, cot_ref, gate_ref, up_ref, down_ref,
    hidden_ref, gpre_ref, sent_ref, gin_ref, garr_ref, gate_grad_ref,
    out_acc, gin_acc, logit_acc,
):
    rows = arr_ref.shape[0]
    step = rows // 3
    t = pl.program_id(0)
    lane = lax.broadcasted_iota(jnp.int32, (step, LANES), 1)

    def shares(logits):
        def softmax(inside):
            held = jnp.where(inside, logits, MASKED)
            raised = jnp.where(
                inside, jnp.exp(held - jnp.max(held, axis=1, keepdims=True)), 0.0
            )
            return raised / jnp.sum(raised, axis=1, keepdims=True)

        def pick(values, at):
            return jnp.sum(jnp.where(lane == at, values, 0.0), axis=1, keepdims=True)

        gates = softmax(lane < experts)
        mixing = softmax((lane >= experts) & (lane < experts + 2))
        return gates, pick(gates, me_ref[0]), pick(mixing, experts), pick(mixing, experts + 1)

    @pl.when(t == 0)
    def _():
        out_acc[...] = jnp.zeros_like(out_acc)
        gin_acc[...] = jnp.zeros_like(gin_acc)
        for low in range(0, rows, step):
            at = slice(low, low + step)
            logits = dot_nn(arr_ref[at, :], gate_ref[...])
            logit_acc[at, :] = logits
            _, chosen, _, mix1 = shares(logits)
            garr_ref[at, :] = ((chosen * mix1) * cot_ref[at, :].astype(f32)).astype(bf16)

    for low in range(0, rows, step):
        at = slice(low, low + step)
        value, slope = gelu_pair(dot_nn(arr_ref[at, :], up_ref[...]))
        h = value.astype(bf16)
        g = (dot_nt(garr_ref[at, :], down_ref[...]) * slope).astype(bf16)
        gpre_ref[at, :] = g
        out_acc[at, :] += dot_nn(h, down_ref[...])
        gin_acc[at, :] += dot_nt(g, up_ref[...])
        hidden_ref[at, :] = h

    @pl.when(t == pl.num_programs(0) - 1)
    def _():
        gate_grad = 0.0
        for low in range(0, rows, step):
            at = slice(low, low + step)
            gates, chosen, mix0, mix1 = shares(logit_acc[at, :])
            out = out_acc[at, :]
            sent_ref[at, :] = ((chosen * mix1) * out).astype(bf16)
            met = jnp.sum(cot_ref[at, :].astype(f32) * out, axis=1, keepdims=True)
            grad_chosen = mix1 * met
            swing = chosen * met * mix0 * mix1
            grad = gates * grad_chosen * (jnp.where(lane == me_ref[0], 1.0, 0.0) - chosen)
            grad = grad + jnp.where(lane == experts + 1, swing, 0.0)
            grad = grad - jnp.where(lane == experts, swing, 0.0)
            low_grad = grad.astype(bf16)
            gin_ref[at, :] = (gin_acc[at, :] + dot_nt(low_grad, gate_ref[...])).astype(bf16)
            gate_grad = gate_grad + dot_nn(grad.T.astype(bf16), arr_ref[at, :])
        gate_grad_ref[...] = gate_grad


def expert(me, arriving, cot, gate_padded, up, down, experts):
    rows, d = arriving.shape
    hidden = up.shape[1]
    width = 512
    columns = pl.BlockSpec((rows, width), lambda t, *_: (0, t))
    return call(
        functools.partial(expert_kernel, experts),
        (hidden // width,),
        [
            fixed((rows, d)),
            fixed((rows, d)),
            fixed((d, LANES)),
            pl.BlockSpec((d, width), lambda t, *_: (0, t)),
            pl.BlockSpec((width, d), lambda t, *_: (t, 0)),
        ],
        [columns, columns] + [kept((rows, d))] * 3 + [kept((LANES, d))],
        [shape_of((rows, hidden), bf16)] * 2
        + [shape_of((rows, d), bf16)] * 3
        + [shape_of((LANES, d), f32)],
        8 * rows * d * hidden,
        scratch=[
            pltpu.VMEM((rows, d), f32),
            pltpu.VMEM((rows, d), f32),
            pltpu.VMEM((rows, LANES), f32),
        ],
        prefetch=1,
        name="expert",
    )(me, arriving, cot, gate_padded, up, down)


def between_kernel(
    target_ref, gin_ref, gs0_ref, gs1_ref, do0_ref, do1_ref, middle_ref, mixing_ref, cot_ref,
    second_ref, mix_t_ref, g_ref, w_ref, gatt_ref, gctx_ref, sums_ref,
):
    @pl.when(pl.program_id(0) == 0)
    def _():
        sums_ref[...] = jnp.zeros_like(sums_ref)

    slots = gin_ref.shape[0]
    lane = lax.broadcasted_iota(jnp.int32, (ROW_BLOCK, slots), 1)
    pick = jnp.where(target_ref[...] == lane, 1.0, 0.0).astype(bf16)
    grad = gs0_ref[...] + gs1_ref[...] + dot_nn(pick, gin_ref[...])
    go = cot_ref[...].astype(f32)
    met = jnp.sum(go * (do0_ref[...] + do1_ref[...]), axis=1, keepdims=True)
    swing = met * mixing_ref[:, 0:1] * mixing_ref[:, 1:2]
    grad = grad + swing * (mix_t_ref[0:1, :] - mix_t_ref[1:2, :])
    n, root = normalized(middle_ref[...])
    sums_ref[0:1, :] += jnp.sum(grad * n, axis=0, keepdims=True)
    sums_ref[1:2, :] += jnp.sum(grad, axis=0, keepdims=True)
    sums_ref[2:3, :] += jnp.sum(second_ref[...].astype(f32) * swing, axis=0, keepdims=True)
    u = grad * g_ref[...]
    u_mean = jnp.mean(u, axis=1, keepdims=True)
    un_mean = jnp.mean(u * n, axis=1, keepdims=True)
    gatt = (go + root * (u - u_mean - n * un_mean)).astype(bf16)
    gatt_ref[...] = gatt
    gctx_ref[...] = dot_nt(gatt, w_ref[...]).astype(bf16)


def between(target, gin, gs, do, middle, mixing, cotangent, second, mix_t, gain, weight):
    rows, d = middle.shape
    slots = gin.shape[0]
    block = rows_of(ROW_BLOCK, d)
    return call(
        between_kernel,
        (rows // ROW_BLOCK,),
        [
            rows_of(ROW_BLOCK, 1), fixed((slots, d)), block, block, block, block, block,
            rows_of(ROW_BLOCK, LANES), block, block, fixed((2, d)), fixed((1, d)), fixed((d, d)),
        ],
        [block, block, kept((8, d))],
        [shape_of((rows, d), bf16), shape_of((rows, d), bf16), shape_of((8, d), f32)],
        2 * rows * d * (d + slots),
        name="between",
    )(
        target, gin, gs[0], gs[1], do[0], do[1], middle, mixing, cotangent, second, mix_t, gain,
        weight,
    )


def out_kernel(target_ref, back_ref, do0_ref, do1_ref, middle_ref, mixing_ref, out_ref):
    slots = back_ref.shape[0]
    lane = lax.broadcasted_iota(jnp.int32, (ROW_BLOCK, slots), 1)
    pick = jnp.where(target_ref[...] == lane, 1.0, 0.0).astype(bf16)
    mixed = mixing_ref[:, 0:1] * (do0_ref[...] + do1_ref[...]) + dot_nn(pick, back_ref[...])
    out_ref[...] = (middle_ref[...] + mixed).astype(bf16)


def outputs_of(target, back, do, middle, mixing):
    rows, d = middle.shape
    slots = back.shape[0]
    block = rows_of(ROW_BLOCK, d)
    return call(
        out_kernel,
        (rows // ROW_BLOCK,),
        [
            rows_of(ROW_BLOCK, 1), fixed((slots, d)), block, block, block,
            rows_of(ROW_BLOCK, LANES),
        ],
        block,
        shape_of((rows, d), bf16),
        2 * rows * d * slots,
        name="outputs",
    )(target, back, do[0], do[1], middle, mixing)


def first_back_kernel(g_ref, w_ref, x_ref, gatt_ref, gain_ref, gx_ref, sums_ref):
    d = x_ref.shape[1]

    @pl.when(pl.program_id(0) == 0)
    def _():
        sums_ref[...] = jnp.zeros_like(sums_ref)

    grad = dot_nt(g_ref[0], w_ref[:, :d])
    grad = grad + dot_nt(g_ref[1], w_ref[:, d : 2 * d])
    grad = grad + dot_nt(g_ref[2], w_ref[:, 2 * d :])
    n, root = normalized(x_ref[...].astype(f32))
    sums_ref[0:1, :] += jnp.sum(grad * n, axis=0, keepdims=True)
    sums_ref[1:2, :] += jnp.sum(grad, axis=0, keepdims=True)
    u = grad * gain_ref[...]
    u_mean = jnp.mean(u, axis=1, keepdims=True)
    un_mean = jnp.mean(u * n, axis=1, keepdims=True)
    gx_ref[...] = (gatt_ref[...].astype(f32) + root * (u - u_mean - n * un_mean)).astype(bf16)


def first_back(grad_qkv, weight, tokens, gatt, gain):
    rows, d = tokens.shape
    block = rows_of(ROW_BLOCK, d)
    return call(
        first_back_kernel,
        (rows // ROW_BLOCK,),
        [
            pl.BlockSpec((3, ROW_BLOCK, d), lambda i: (0, i, 0)),
            fixed((d, 3 * d)),
            block,
            block,
            fixed((1, d)),
        ],
        [block, kept((8, d))],
        [shape_of((rows, d), bf16), shape_of((8, d), f32)],
        6 * rows * d * d,
        name="first_back",
    )(grad_qkv, weight, tokens, gatt, gain)


def expert_grad_kernel(owner_ref, a_ref, b_ref, out_ref):
    out_ref[0] = dot_nn(a_ref[...], b_ref[...]).astype(bf16)


def up_grad(owners, a, b, n):
    d, rows = a.shape
    width = b.shape[1] // n
    m = owners.shape[0]
    return call(
        expert_grad_kernel,
        (m,),
        [fixed((d, rows)), pl.BlockSpec((rows, width), lambda t, owner: (0, owner[t]))],
        pl.BlockSpec((1, d, width), lambda t, owner: (t, 0, 0)),
        shape_of((m, d, width), bf16),
        2 * rows * d * width * m,
        prefetch=1,
        name="up_grad",
    )(owners, a, b)


def down_grad_kernel(owner_ref, a_ref, b_ref, out_ref):
    out_ref[0] = lax.dot_general(
        a_ref[...], b_ref[...], (((0,), (0,)), ((), ())), preferred_element_type=f32
    ).astype(bf16)


def down_grad(owners, a, b, n):
    rows, d = b.shape
    width = a.shape[1] // n
    m = owners.shape[0]
    return call(
        down_grad_kernel,
        (m,),
        [pl.BlockSpec((rows, width), lambda t, owner: (0, owner[t])), fixed((rows, d))],
        pl.BlockSpec((1, width, d), lambda t, owner: (t, 0, 0)),
        shape_of((m, width, d), bf16),
        2 * rows * d * width * m,
        prefetch=1,
        name="down_grad",
    )(owners, a, b)


def swap(values, axis, bit):
    n = lax.axis_size(axis)
    return lax.ppermute(values, axis, [(i, i ^ bit) for i in range(n)])


def plus(a, b):
    return (a.astype(f32) + b.astype(f32)).astype(bf16)


def halve(keep, send, axis, bits):
    summed = plus(keep, swap(send, axis, bits[0]))
    if len(bits) == 1:
        return summed
    m = summed.shape[0] // 2
    return halve(summed[:m], summed[m:], axis, bits[1:])


def halve_absolute(values, axis, bits, me):
    for bit in bits:
        m = values.shape[0] // 2
        axis_at = 0 if bits[0] >= bits[-1] else 1
        split = values.reshape(((2, m), (m, 2))[axis_at] + values.shape[1:])
        mine = (me // bit) % 2
        keep = lax.dynamic_index_in_dim(split, mine, axis_at, keepdims=False)
        send = lax.dynamic_index_in_dim(split, 1 - mine, axis_at, keepdims=False)
        values = plus(keep, swap(send, axis, bit))
    return values[0]


def reversed_bits(value, count):
    return sum(((value >> i) & 1) << (count - 1 - i) for i in range(count))


def shards(
    tokens, lengths, key_mask, routes, norm1_gain, norm1_bias, qkv_weight, out_weight,
    norm2_gain, norm2_bias, up_weight, down_weight, router_weight, mix_weight, expert_up,
    expert_down, cotangent,
):
    rows, d = tokens.shape
    groups, copies = lax.axis_size("ep"), lax.axis_size("dp")
    experts = expert_up.shape[0] * groups
    capacity = (5 * rows + 4 * experts - 1) // (4 * experts)
    slots = experts * capacity
    ep, dp = lax.axis_index("ep"), lax.axis_index("dp")
    core, level, levels = ep % 2, ep // 2, groups // 2
    count = copies.bit_length() - 1
    up_bits = [1 << i for i in reversed(range(count))]
    down_bits = [1 << i for i in range(count)]
    level_groups = [[2 * z + c for z in range(levels)] for c in range(2)]
    order = jnp.arange(copies, dtype=jnp.int32)
    back_order = jnp.array([reversed_bits(t, count) for t in range(copies)], jnp.int32)
    owners = dp.astype(jnp.int32) ^ order
    back_owners = dp.astype(jnp.int32) ^ back_order
    core_scalar = core.astype(jnp.int32).reshape(1)

    row_at = jnp.arange(rows, dtype=jnp.int32)
    live = row_at < lengths[0]
    flat_routes = routes[:, 0]
    routed = (flat_routes[:, None] == jnp.arange(experts)[None, :]) & live[:, None]
    ahead = dot_nn(
        (row_at[None, :] < row_at[:, None]).astype(bf16), routed.astype(bf16)
    )
    place = jnp.sum(jnp.where(routed, ahead, 0.0), axis=1).astype(jnp.int32)
    target = jnp.where(live, flat_routes * capacity + place, slots)
    target_column = target[:, None]
    pick = (jnp.arange(slots, dtype=jnp.int32)[:, None] == target[None, :]).astype(bf16)

    def exchange(values):
        return lax.all_to_all(
            values.reshape(groups, slots // groups, d), "ep", 0, 0, tiled=True
        ).reshape(slots, d)

    def dispatch(values):
        return exchange(dot_nn(pick, values).astype(bf16))

    cot_arriving = dispatch(cotangent)
    usable = live & (key_mask == 1)
    bias = jnp.where(usable, 0.0, MASKED).astype(f32)[:, None]
    first, qkv = ln_qkv(tokens, norm1_gain[None], norm1_bias[None], qkv_weight)
    context, context_t, lse = attend(qkv, bias)
    mix_padded = jnp.pad(mix_weight, ((0, 0), (0, LANES - 2)))
    gate_padded = jnp.pad(
        jnp.concatenate([router_weight, mix_weight], axis=1),
        ((0, 0), (0, LANES - 2 - experts)),
    )
    middle, second, second_t, gdl, gdl_t, mixing = after(
        core_scalar, tokens, context, cotangent, out_weight, norm2_gain[None], norm2_bias[None],
        mix_padded, d // groups,
    )
    arriving = dispatch(second)

    dense_parts = [
        dense(chunk, owners, back_order, second, second_t, gdl, gdl_t, up_weight, down_weight)
        for chunk in range(CHUNKS)
    ]
    dense_out = [part[0] for part in dense_parts]
    grad_second = [part[1] for part in dense_parts]
    up_pieces, down_pieces = [], []
    m = copies // 2
    for _, _, up_keep, up_send, down_keep, down_send in dense_parts:
        up_pair = plus(up_keep, swap(up_send, "ep", 1))
        down_pair = plus(down_keep, swap(down_send, "ep", 1))
        up_pieces.append(halve(up_pair[:m], up_pair[m:], "dp", up_bits)[0])
        down_pieces.append(halve(down_pair[:m], down_pair[m:], "dp", down_bits)[0])
    dense_square = jnp.stack(
        [jnp.concatenate(up_pieces, axis=1), jnp.concatenate(down_pieces, axis=1)]
    ).reshape(2, levels, d // groups, -1)
    dense_sum = lax.psum_scatter(
        dense_square.transpose(1, 0, 2, 3), "ep", scatter_dimension=0, tiled=True,
        axis_index_groups=level_groups,
    )[0].astype(f32)
    up_sum, down_sum = dense_sum[0], dense_sum[1].T

    hidden, gpre, sent, gin, garr, gate_grad = expert(
        ep.astype(jnp.int32).reshape(1), arriving, cot_arriving, gate_padded, expert_up[0],
        expert_down[0], experts,
    )
    grad_back = exchange(gin)
    expert_back = exchange(sent)
    arriving_t = arriving.T
    up_send = up_grad(owners[m:], arriving_t, gpre, copies)
    down_send = down_grad(back_owners[m:], hidden, garr, copies)
    up_keep = up_grad(owners[:m], arriving_t, gpre, copies)
    down_keep = down_grad(back_owners[:m], hidden, garr, copies)
    expert_up_sum = halve(up_keep, up_send, "dp", up_bits).astype(f32)
    expert_down_sum = halve(down_keep, down_send, "dp", down_bits).astype(f32)

    gatt, grad_context, sums2 = between(
        target_column, grad_back, grad_second, dense_out, middle, mixing, cotangent, second,
        mix_weight.T.astype(f32), norm2_gain[None], out_weight,
    )
    outputs = outputs_of(target_column, expert_back, dense_out, middle, mixing)

    def owned(values, me_dp):
        height = values.shape[0] // (copies * groups)
        split = values.reshape(copies, levels, 2, height, -1)
        keep = lax.dynamic_index_in_dim(split, core, 2, keepdims=False)
        send = lax.dynamic_index_in_dim(split, 1 - core, 2, keepdims=False)
        pair = plus(keep, swap(send, "ep", 1))
        half = pair.shape[-1] // 2
        left = halve_absolute(pair[..., :half], "dp", up_bits, me_dp)
        right = halve_absolute(pair[..., half:], "dp", down_bits, me_dp)
        whole = jnp.concatenate([left, right], axis=-1)
        return lax.psum_scatter(
            whole, "ep", scatter_dimension=0, tiled=True, axis_index_groups=level_groups
        )[0].astype(f32)

    out_sum = owned(dot_nn(context_t, gatt).astype(bf16), dp)
    grad_qkv, grad_qkv_t = attend_back(qkv, bias, lse, grad_context)
    grad_inputs, sums1 = first_back(grad_qkv, qkv_weight, tokens, gatt, norm1_gain[None])
    qkv_sum = owned(dot_nn(grad_qkv_t.reshape(3 * d, rows), first).astype(bf16), dp).T

    home_mix = jnp.concatenate(
        [jnp.zeros((experts, d), f32), sums2[2:3], -sums2[2:3]], axis=0
    )
    small = jnp.concatenate(
        [sums1[:2], sums2[:2], gate_grad[: experts + 2] + home_mix], axis=0
    )
    small = lax.psum_scatter(small.T, ("dp", "ep"), scatter_dimension=0, tiled=True)
    return (
        outputs, grad_inputs, small[:, 0], small[:, 1], qkv_sum, out_sum, small[:, 2],
        small[:, 3], up_sum, down_sum, small[:, 4 : 4 + experts], small[:, 4 + experts :],
        expert_up_sum, expert_down_sum,
    )


def solution(mesh):
    split = ("dp", "ep")
    return jax.shard_map(
        shards,
        mesh=mesh,
        in_specs=(
            P(split, None), P(split), P(split), P(split, None), P(), P(), P(), P(), P(), P(),
            P(), P(), P(), P(), P("ep", None, None), P("ep", None, None), P(split, None),
        ),
        out_specs=(
            P(split, None), P(split, None), P(split), P(split), P(None, split), P(split, None),
            P(split), P(split), P("ep", "dp"), P("dp", "ep"), P(split, None), P(split, None),
            P("ep", None, "dp"), P("ep", "dp", None),
        ),
        check_vma=False,
    )
```

```python
import functools

import jax
import jax.numpy as jnp
from jax import lax
from jax.experimental import pallas as pl
from jax.experimental.pallas import tpu as pltpu
from jax.sharding import PartitionSpec as P

HEAD_DIM = 64
EPSILON = 1e-05
MASKED = -1e30
ROW_BLOCK = 256
CHUNKS = 2
WEIGHT = 0.01
LANES = 128
GELU_ROOT = 0.7978845608028654
GELU_CUBE = 0.044715

f32 = jnp.float32
bf16 = jnp.bfloat16


def dot_nn(a, b):
    return lax.dot_general(a, b, (((1,), (0,)), ((), ())), preferred_element_type=f32)


def dot_nt(a, b):
    return lax.dot_general(a, b, (((1,), (1,)), ((), ())), preferred_element_type=f32)


class Line:
    last = None
    others = ()

    @classmethod
    def run(cls, function, *values):
        result = function(*values)
        cls.last = jax.tree.leaves(result)[0]
        return result


def call(kernel, grid, in_specs, out_specs, out_shape, micros, scratch=(), prefetch=0, name=None):
    def apply(*operands):
        specs, count, ordered = list(in_specs), len(operands), kernel
        if Line.last is not None:
            unread = (Line.last,) + Line.others
            Line.others = ()
            specs += [pl.BlockSpec(memory_space=pl.ANY)] * len(unread)
            operands += unread

            def ordered(*refs):
                kernel(*refs[:count], *refs[count + len(unread) :])

        return pl.pallas_call(
            ordered,
            grid_spec=pltpu.PrefetchScalarGridSpec(
                num_scalar_prefetch=prefetch,
                grid=grid,
                in_specs=specs,
                out_specs=out_specs,
                scratch_shapes=list(scratch),
            ),
            out_shape=out_shape,
            compiler_params=pltpu.CompilerParams(
                dimension_semantics=("arbitrary",) * len(grid), vmem_limit_bytes=56 * 1024 * 1024
            ),
            cost_estimate=pl.CostEstimate(
                flops=int(micros * WEIGHT * 1.15e9),
                bytes_accessed=int(micros * WEIGHT * 3e6),
                transcendentals=0,
            ),
            name=name,
        )(*operands)

    return apply


def fixed(shape):
    return pl.BlockSpec(
        shape, lambda *_: (0,) * len(shape), pipeline_mode=pl.Buffered(buffer_count=1)
    )


def kept(shape):
    return pl.BlockSpec(shape, lambda *_: (0,) * len(shape))


def rows_of(height, width):
    return pl.BlockSpec((height, width), lambda i, *_: (i, 0))


def shape_of(shape, dtype):
    return jax.ShapeDtypeStruct(shape, dtype)


def normalized(values):
    average = jnp.mean(values, axis=1, keepdims=True)
    centered = values - average
    root = lax.rsqrt(jnp.mean(centered * centered, axis=1, keepdims=True) + EPSILON)
    return centered * root, root


def gelu_pair(v):
    square = v * v
    t = jnp.tanh(v * (GELU_ROOT + (GELU_ROOT * GELU_CUBE) * square))
    half = 0.5 + 0.5 * t
    slope = half + (v * (0.5 - 0.5 * (t * t))) * (
        GELU_ROOT + (3.0 * GELU_ROOT * GELU_CUBE) * square
    )
    return v * half, slope


def ln_qkv_kernel(x_ref, g_ref, b_ref, w_ref, first_ref, qkv_ref):
    @pl.when(pl.program_id(0) == 0)
    def _():
        def some_rows(i, carry):
            at = pl.ds(pl.multiple_of(i * LANES, LANES), LANES)
            n, _ = normalized(x_ref[at, :].astype(f32))
            first_ref[at, :] = (n * g_ref[...] + b_ref[...]).astype(bf16)
            return carry

        lax.fori_loop(0, x_ref.shape[0] // LANES, some_rows, 0)

    qkv_ref[...] = dot_nn(first_ref[...], w_ref[...]).astype(bf16)


def ln_qkv(tokens, gain, bias, weight):
    rows, d = tokens.shape
    width = weight.shape[1]
    block = 512
    return call(
        ln_qkv_kernel,
        (width // block,),
        [
            fixed((rows, d)),
            fixed((1, d)),
            fixed((1, d)),
            pl.BlockSpec((d, block), lambda i: (0, i)),
        ],
        [kept((rows, d)), pl.BlockSpec((rows, block), lambda i: (0, i))],
        [shape_of((rows, d), bf16), shape_of((rows, width), bf16)],
        micros=11,
        name="ln_qkv",
    )(tokens, gain, bias, weight)


def diagonal_bias(bias_rows):
    size = bias_rows.shape[0]
    key_at = lax.broadcasted_iota(jnp.int32, (size, size), 0)
    query_at = lax.broadcasted_iota(jnp.int32, (size, size), 1)
    return jnp.where(
        key_at == query_at, 0.0, jnp.where(key_at < query_at, bias_rows, MASKED)
    )


def head_lanes(values, head):
    lane = lax.broadcasted_iota(jnp.int32, values.shape, 1)
    inside = (lane >= head * HEAD_DIM) & (lane < (head + 1) * HEAD_DIM)
    return jnp.where(inside, values, jnp.zeros_like(values))


def attend_kernel(bias_ref, q_ref, k_ref, v_ref, ctx_ref, ctx_t_ref, lse_ref):
    rows = q_ref.shape[0]
    v_t = v_ref[...].T
    for i in range(rows // ROW_BLOCK):
        low, high = i * ROW_BLOCK, (i + 1) * ROW_BLOCK
        edge = diagonal_bias(bias_ref[low:high, :])
        q = q_ref[low:high, :] * jnp.asarray(HEAD_DIM**-0.5, bf16)
        sides = []
        for head in range(2):
            q_head = head_lanes(q, head)
            inner = dot_nt(k_ref[low:high, :], q_head) + edge
            top = jnp.max(inner, axis=0, keepdims=True)
            if i:
                outer = dot_nt(k_ref[:low, :], q_head) + bias_ref[:low, :]
                top = jnp.maximum(top, jnp.max(outer, axis=0, keepdims=True))
            inner = jnp.exp(inner - top)
            total = jnp.sum(inner, axis=0, keepdims=True)
            v_head = v_t[head * HEAD_DIM : (head + 1) * HEAD_DIM, :]
            side = dot_nn(v_head[:, low:high], inner.astype(bf16))
            if i:
                outer = jnp.exp(outer - top)
                total = total + jnp.sum(outer, axis=0, keepdims=True)
                side = side + dot_nn(v_head[:, :low], outer.astype(bf16))
            sides.append(side / total)
            lse_ref[0, head : head + 1, low:high] = top + jnp.log(total)
        both = jnp.concatenate(sides, axis=0)
        ctx_t_ref[:, low:high] = both.astype(bf16)
        ctx_ref[low:high, :] = both.T.astype(bf16)


def attend(qkv, bias):
    rows, d = qkv.shape[0], qkv.shape[1] // 3
    pairs = d // LANES

    def third(n):
        return pl.BlockSpec((rows, LANES), lambda h: (0, n * pairs + h))

    return call(
        attend_kernel,
        (pairs,),
        [fixed((rows, 1)), third(0), third(1), third(2)],
        [
            third(0),
            pl.BlockSpec((LANES, rows), lambda h: (h, 0)),
            pl.BlockSpec((1, 8, rows), lambda h: (h, 0, 0)),
        ],
        [
            shape_of((rows, d), bf16),
            shape_of((d, rows), bf16),
            shape_of((pairs, 8, rows), f32),
        ],
        micros=22,
        name="attend",
    )(bias, qkv, qkv, qkv)


def attend_back_kernel(
    bias_ref, lse_ref, q_ref, k_ref, v_ref, do_ref, g_ref, g_t_ref, gk_acc, gv_acc
):
    rows = q_ref.shape[0]
    scale = HEAD_DIM**-0.5
    k_t = k_ref[...].T
    gk_acc[...] = jnp.zeros_like(gk_acc)
    gv_acc[...] = jnp.zeros_like(gv_acc)
    for i in range(rows // ROW_BLOCK):
        low, high = i * ROW_BLOCK, (i + 1) * ROW_BLOCK
        edge = diagonal_bias(bias_ref[low:high, :])
        q = q_ref[low:high, :] * jnp.asarray(scale, bf16)
        do = do_ref[low:high, :]
        sides = []
        for head in range(2):
            q_head = head_lanes(q, head)
            do_head = head_lanes(do, head)
            lse = lse_ref[0, head : head + 1, low:high]
            spans = [(low, high, edge)]
            if i:
                spans.append((0, low, bias_ref[:low, :]))
            probs, grads = [], []
            dots = 0.0
            for start, stop, bias in spans:
                p = jnp.exp(dot_nt(k_ref[start:stop, :], q_head) + bias - lse)
                gp = dot_nt(v_ref[start:stop, :], do_head)
                dots = dots + jnp.sum(p * gp, axis=0, keepdims=True)
                probs.append(p)
                grads.append(gp)
            side = 0.0
            k_head = k_t[head * HEAD_DIM : (head + 1) * HEAD_DIM, :]
            for (start, stop, _), p, gp in zip(spans, probs, grads):
                ds = (p * (gp - dots)).astype(bf16)
                gv_acc[start:stop, :] += dot_nn(p.astype(bf16), do_head)
                gk_acc[start:stop, :] += dot_nn(ds, q_head)
                side = side + dot_nn(k_head[:, start:stop], ds)
            sides.append(side * scale)
        both = jnp.concatenate(sides, axis=0)
        g_t_ref[0, :, low:high] = both.astype(bf16)
        g_ref[0, low:high, :] = both.T.astype(bf16)
    for n, acc in ((1, gk_acc), (2, gv_acc)):
        g_ref[n] = acc[...].astype(bf16)
        g_t_ref[n] = acc[...].T.astype(bf16)


def attend_back(qkv, bias, lse, grad_context):
    rows, d = grad_context.shape
    pairs = d // LANES

    def third(n):
        return pl.BlockSpec((rows, LANES), lambda h: (0, n * pairs + h))

    return call(
        attend_back_kernel,
        (pairs,),
        [
            fixed((rows, 1)),
            pl.BlockSpec((1, 8, rows), lambda h: (h, 0, 0)),
            third(0),
            third(1),
            third(2),
            third(0),
        ],
        [
            pl.BlockSpec((3, rows, LANES), lambda h: (0, 0, h)),
            pl.BlockSpec((3, LANES, rows), lambda h: (0, h, 0)),
        ],
        [shape_of((3, rows, d), bf16), shape_of((3, d, rows), bf16)],
        scratch=[pltpu.VMEM((rows, LANES), f32), pltpu.VMEM((rows, LANES), f32)],
        micros=28,
        name="attend_back",
    )(bias, lse, qkv, qkv, qkv, grad_context)


def after_kernel(
    rb, core_ref, x_ref, ctx_ref, cot_ref, w_ref, g_ref, b_ref, mix_ref,
    middle_ref, second_ref, second_t_ref, gdl_ref, gdl_t_ref, mixing_ref,
):
    d = x_ref.shape[1]
    middle = x_ref[...].astype(f32) + dot_nn(ctx_ref[...], w_ref[...])
    middle_ref[...] = middle
    n, _ = normalized(middle)
    second = (n * g_ref[...] + b_ref[...]).astype(bf16)
    second_ref[...] = second
    logits = dot_nn(second, mix_ref[...])
    gap = logits[:, 1:2] - logits[:, 0:1]
    first_share = 1.0 / (1.0 + jnp.exp(gap))
    other_share = 1.0 / (1.0 + jnp.exp(-gap))
    lane = lax.broadcasted_iota(jnp.int32, mixing_ref.shape, 1)
    mixing_ref[...] = jnp.where(lane == 0, first_share, other_share)
    gdl = (first_share * cot_ref[...].astype(f32)).astype(bf16)
    gdl_ref[...] = gdl
    core = core_ref[0]
    for values, target in ((second, second_t_ref), (gdl, gdl_t_ref)):
        turned = values.astype(f32).T.astype(bf16)
        for piece in range(d // rb):
            place = ((piece % 2) ^ core) * (d // (2 * rb)) + piece // 2
            target[pl.ds(pl.multiple_of(place * rb, rb), rb), :] = turned[
                piece * rb : (piece + 1) * rb, :
            ]


def after(tokens, core, context, cotangent, weight, gain, bias, mix_padded, rb):
    rows, d = tokens.shape
    block = rows_of(ROW_BLOCK, d)
    turned = pl.BlockSpec((d, ROW_BLOCK), lambda i, *_: (0, i))
    return call(
        functools.partial(after_kernel, rb),
        (rows // ROW_BLOCK,),
        [block, block, block, fixed((d, d)), fixed((1, d)), fixed((1, d)), fixed((d, LANES))],
        [block, block, turned, block, turned, rows_of(ROW_BLOCK, LANES)],
        [
            shape_of((rows, d), f32),
            shape_of((rows, d), bf16),
            shape_of((d, rows), bf16),
            shape_of((rows, d), bf16),
            shape_of((d, rows), bf16),
            shape_of((rows, LANES), f32),
        ],
        prefetch=1,
        micros=10,
        name="after",
    )(core, tokens, context, cotangent, weight, gain, bias, mix_padded)


def dense_kernel(
    owner_ref, second_ref, second_t_ref, gdl_ref, gdl_t_ref, up_ref, down_ref,
    hidden_ref, gpre_ref, keep_ref, send_ref, keep_next_ref, send_next_ref,
):
    rows = second_ref.shape[0]
    half = second_t_ref.shape[0] // 2
    levels = keep_ref.shape[1]
    for low in range(0, rows, ROW_BLOCK):
        at = slice(low, low + ROW_BLOCK)
        value, slope = gelu_pair(dot_nn(second_ref[at, :], up_ref[...]))
        hidden_ref[0, at, :] = value.astype(bf16)
        gpre_ref[0, at, :] = (dot_nt(gdl_ref[at, :], down_ref[...]) * slope).astype(bf16)

    def write(keep, send):
        for n, lhs_ref, units_ref in ((0, second_t_ref, gpre_ref), (1, gdl_t_ref, hidden_ref)):
            for target, low in ((keep, 0), (send, half)):
                grad = dot_nn(lhs_ref[low : low + half, :], units_ref[0]).astype(bf16)
                for z in range(levels):
                    target[0, z, n] = grad[z * (half // levels) : (z + 1) * (half // levels)]

    upper = pl.program_id(0) >= pl.num_programs(0) // 2
    pl.when(jnp.logical_not(upper))(lambda: write(keep_ref, send_ref))
    pl.when(upper)(lambda: write(keep_next_ref, send_next_ref))


def dense(second, chunk, owners, levels, second_t, gdl, gdl_t, up, down):
    rows, d = second.shape
    n = owners.shape[0]
    width = up.shape[1] // (n * CHUNKS)
    shape = (levels, 2, d // (2 * levels), width)
    lower = pl.BlockSpec((1,) + shape, lambda t, _: (jnp.minimum(t, n // 2 - 1), 0, 0, 0, 0))
    upper = pl.BlockSpec((1,) + shape, lambda t, _: (jnp.maximum(t - n // 2, 0), 0, 0, 0, 0))
    units = pl.BlockSpec((1, rows, width), lambda t, _: (t, 0, 0))
    return call(
        dense_kernel,
        (n,),
        [
            fixed((rows, d)),
            fixed((d, rows)),
            fixed((rows, d)),
            fixed((d, rows)),
            pl.BlockSpec((d, width), lambda t, owner: (0, owner[t] * CHUNKS + chunk)),
            pl.BlockSpec((width, d), lambda t, owner: (owner[t] * CHUNKS + chunk, 0)),
        ],
        [units, units, lower, lower, upper, upper],
        [shape_of((n, rows, width), bf16)] * 2
        + [shape_of((n // 2,) + shape, bf16)] * 4,
        prefetch=1,
        micros=100,
        name="dense",
    )(owners, second, second_t, gdl, gdl_t, up, down)


def dense_rest_kernel(
    owner_ref, place_ref, hidden0_ref, hidden1_ref, gpre0_ref, gpre1_ref, up_ref, down_ref,
    out_ref, gsec_ref,
):
    width = hidden0_ref.shape[2]

    @pl.when(pl.program_id(0) == 0)
    def _():
        out_ref[...] = jnp.zeros_like(out_ref)
        gsec_ref[...] = jnp.zeros_like(gsec_ref)

    out_ref[...] += dot_nn(hidden0_ref[0], down_ref[:width, :]) + dot_nn(
        hidden1_ref[0], down_ref[width:, :]
    )
    gsec_ref[...] += dot_nt(gpre0_ref[0], up_ref[:, :width]) + dot_nt(
        gpre1_ref[0], up_ref[:, width:]
    )


def dense_rest(hidden0, owners, places, hidden1, gpre0, gpre1, up, down):
    n, rows, width = hidden0.shape
    d = up.shape[0]
    units0 = pl.BlockSpec((1, rows, width), lambda t, owner, place: (t, 0, 0))
    units1 = pl.BlockSpec((1, rows, width), lambda t, owner, place: (place[t], 0, 0))
    return call(
        dense_rest_kernel,
        (n,),
        [
            units0,
            units1,
            units0,
            units1,
            pl.BlockSpec((d, 2 * width), lambda t, owner, _: (0, owner[t])),
            pl.BlockSpec((2 * width, d), lambda t, owner, _: (owner[t], 0)),
        ],
        [kept((rows, d))] * 2,
        [shape_of((rows, d), f32)] * 2,
        prefetch=2,
        micros=3000,
        name="dense_rest",
    )(owners, places, hidden0, hidden1, gpre0, gpre1, up, down)


def shares(logits, experts, me):
    lane = lax.broadcasted_iota(jnp.int32, logits.shape, 1)

    def softmax(inside):
        held = jnp.where(inside, logits, MASKED)
        raised = jnp.where(inside, jnp.exp(held - jnp.max(held, axis=1, keepdims=True)), 0.0)
        return raised / jnp.sum(raised, axis=1, keepdims=True)

    def pick(values, at):
        return jnp.sum(jnp.where(lane == at, values, 0.0), axis=1, keepdims=True)

    gates = softmax(lane < experts)
    mixing = softmax((lane >= experts) & (lane < experts + 2))
    return gates, pick(gates, me), pick(mixing, experts), pick(mixing, experts + 1)


def expert_step(arr_ref, garr_ref, up_ref, down_ref, hidden_ref, gpre_ref, out_acc, gin_acc):
    rows = arr_ref.shape[0]
    step = rows // 3
    for low in range(0, rows, step):
        at = slice(low, low + step)
        value, slope = gelu_pair(dot_nn(arr_ref[at, :], up_ref[...]))
        h = value.astype(bf16)
        g = (dot_nt(garr_ref[at, :], down_ref[...]) * slope).astype(bf16)
        gpre_ref[0, at, :] = g
        out_acc[at, :] += dot_nn(h, down_ref[...])
        gin_acc[at, :] += dot_nt(g, up_ref[...])
        hidden_ref[0, at, :] = h


def expert_first_kernel(
    experts, me_ref, arr_ref, cot_ref, gate_ref, up_ref, down_ref,
    hidden_ref, gpre_ref, garr_ref, logit_ref, out_acc, gin_acc,
):
    rows = arr_ref.shape[0]
    step = rows // 3

    @pl.when(pl.program_id(0) == 0)
    def _():
        out_acc[...] = jnp.zeros_like(out_acc)
        gin_acc[...] = jnp.zeros_like(gin_acc)
        for low in range(0, rows, step):
            at = slice(low, low + step)
            logits = dot_nn(arr_ref[at, :], gate_ref[...])
            logit_ref[at, :] = logits
            _, chosen, _, mix1 = shares(logits, experts, me_ref[0])
            garr_ref[at, :] = ((chosen * mix1) * cot_ref[at, :].astype(f32)).astype(bf16)

    expert_step(arr_ref, garr_ref, up_ref, down_ref, hidden_ref, gpre_ref, out_acc, gin_acc)


def expert_second_kernel(
    experts, me_ref, arr_ref, cot_ref, gate_ref, up_ref, down_ref, garr_ref, logit_ref, out_ref,
    grad_ref, hidden_ref, gpre_ref, sent_ref, gin_ref, gate_grad_ref, out_acc, gin_acc,
):
    rows = arr_ref.shape[0]
    step = rows // 3
    me = me_ref[0]

    @pl.when(pl.program_id(0) == 0)
    def _():
        out_acc[...] = out_ref[...]
        gin_acc[...] = grad_ref[...]

    expert_step(arr_ref, garr_ref, up_ref, down_ref, hidden_ref, gpre_ref, out_acc, gin_acc)

    @pl.when(pl.program_id(0) == pl.num_programs(0) - 1)
    def _():
        gate_grad = 0.0
        lane = lax.broadcasted_iota(jnp.int32, (step, LANES), 1)
        for low in range(0, rows, step):
            at = slice(low, low + step)
            gates, chosen, mix0, mix1 = shares(logit_ref[at, :], experts, me)
            out = out_acc[at, :]
            sent_ref[at, :] = ((chosen * mix1) * out).astype(bf16)
            met = jnp.sum(cot_ref[at, :].astype(f32) * out, axis=1, keepdims=True)
            grad_chosen = mix1 * met
            swing = chosen * met * mix0 * mix1
            grad = gates * grad_chosen * (jnp.where(lane == me, 1.0, 0.0) - chosen)
            grad = grad + jnp.where(lane == experts + 1, swing, 0.0)
            grad = grad - jnp.where(lane == experts, swing, 0.0)
            low_grad = grad.astype(bf16)
            gin_ref[at, :] = (gin_acc[at, :] + dot_nt(low_grad, gate_ref[...])).astype(bf16)
            gate_grad = gate_grad + dot_nn(grad.T.astype(bf16), arr_ref[at, :])
        gate_grad_ref[...] = gate_grad


def expert(arriving, half, n, me, cot, gate_padded, up, down, experts, before=None):
    rows, d = arriving.shape
    width = up.shape[1] // (2 * n)
    units = pl.BlockSpec((1, rows, width), lambda t, *_: (t, 0, 0))
    specs = [
        fixed((rows, d)),
        fixed((rows, d)),
        fixed((d, LANES)),
        pl.BlockSpec((d, width), lambda t, *_: (0, 2 * t + half)),
        pl.BlockSpec((width, d), lambda t, *_: (2 * t + half, 0)),
    ]
    shapes = [shape_of((n, rows, width), bf16)] * 2
    if half == 0:
        return call(
            functools.partial(expert_first_kernel, experts),
            (n,),
            specs,
            [units, units] + [kept((rows, d)), kept((rows, LANES))] + [kept((rows, d))] * 2,
            shapes
            + [shape_of((rows, d), bf16), shape_of((rows, LANES), f32)]
            + [shape_of((rows, d), f32)] * 2,
            prefetch=1,
            micros=4800,
            name="expert_first",
        )(me, arriving, cot, gate_padded, up, down)
    return call(
        functools.partial(expert_second_kernel, experts),
        (n,),
        specs + [fixed((rows, d)), fixed((rows, LANES)), fixed((rows, d)), fixed((rows, d))],
        [units, units] + [kept((rows, d))] * 2 + [kept((LANES, d))],
        shapes + [shape_of((rows, d), bf16)] * 2 + [shape_of((LANES, d), f32)],
        scratch=[pltpu.VMEM((rows, d), f32), pltpu.VMEM((rows, d), f32)],
        prefetch=1,
        micros=100,
        name="expert_second",
    )(me, arriving, cot, gate_padded, up, down, *before)


def between_kernel(
    target_ref, gin_ref, gs_ref, do_ref, middle_ref, mixing_ref, cot_ref,
    second_ref, mix_t_ref, g_ref, w_ref, gatt_ref, gctx_ref, sums_ref,
):
    @pl.when(pl.program_id(0) == 0)
    def _():
        sums_ref[...] = jnp.zeros_like(sums_ref)

    slots = gin_ref.shape[0]
    lane = lax.broadcasted_iota(jnp.int32, (ROW_BLOCK, slots), 1)
    pick = jnp.where(target_ref[...] == lane, 1.0, 0.0).astype(bf16)
    grad = gs_ref[...] + dot_nn(pick, gin_ref[...])
    go = cot_ref[...].astype(f32)
    met = jnp.sum(go * do_ref[...], axis=1, keepdims=True)
    swing = met * mixing_ref[:, 0:1] * mixing_ref[:, 1:2]
    grad = grad + swing * (mix_t_ref[0:1, :] - mix_t_ref[1:2, :])
    n, root = normalized(middle_ref[...])
    sums_ref[0:1, :] += jnp.sum(grad * n, axis=0, keepdims=True)
    sums_ref[1:2, :] += jnp.sum(grad, axis=0, keepdims=True)
    sums_ref[2:3, :] += jnp.sum(second_ref[...].astype(f32) * swing, axis=0, keepdims=True)
    u = grad * g_ref[...]
    u_mean = jnp.mean(u, axis=1, keepdims=True)
    un_mean = jnp.mean(u * n, axis=1, keepdims=True)
    gatt = (go + root * (u - u_mean - n * un_mean)).astype(bf16)
    gatt_ref[...] = gatt
    gctx_ref[...] = dot_nt(gatt, w_ref[...]).astype(bf16)


def between(gs, target, gin, do, middle, mixing, cotangent, second, mix_t, gain, weight):
    rows, d = middle.shape
    slots = gin.shape[0]
    block = rows_of(ROW_BLOCK, d)
    return call(
        between_kernel,
        (rows // ROW_BLOCK,),
        [
            rows_of(ROW_BLOCK, 1), fixed((slots, d)), block, block, block,
            rows_of(ROW_BLOCK, LANES), block, block, fixed((2, d)), fixed((1, d)), fixed((d, d)),
        ],
        [block, block, kept((8, d))],
        [shape_of((rows, d), bf16), shape_of((rows, d), bf16), shape_of((8, d), f32)],
        micros=12,
        name="between",
    )(
        target, gin, gs, do, middle, mixing, cotangent, second, mix_t, gain,
        weight,
    )


def out_kernel(target_ref, back_ref, do_ref, middle_ref, mixing_ref, out_ref):
    slots = back_ref.shape[0]
    lane = lax.broadcasted_iota(jnp.int32, (ROW_BLOCK, slots), 1)
    pick = jnp.where(target_ref[...] == lane, 1.0, 0.0).astype(bf16)
    mixed = mixing_ref[:, 0:1] * do_ref[...] + dot_nn(pick, back_ref[...])
    out_ref[...] = (middle_ref[...] + mixed).astype(bf16)


def outputs_of(do, target, back, middle, mixing):
    rows, d = middle.shape
    slots = back.shape[0]
    block = rows_of(ROW_BLOCK, d)
    return call(
        out_kernel,
        (rows // ROW_BLOCK,),
        [
            rows_of(ROW_BLOCK, 1), fixed((slots, d)), block, block,
            rows_of(ROW_BLOCK, LANES),
        ],
        block,
        shape_of((rows, d), bf16),
        micros=7,
        name="outputs",
    )(target, back, do, middle, mixing)


def first_back_kernel(g_ref, w_ref, x_ref, gatt_ref, gain_ref, gx_ref, sums_ref):
    d = x_ref.shape[1]

    @pl.when(pl.program_id(0) == 0)
    def _():
        sums_ref[...] = jnp.zeros_like(sums_ref)

    grad = dot_nt(g_ref[0], w_ref[:, :d])
    grad = grad + dot_nt(g_ref[1], w_ref[:, d : 2 * d])
    grad = grad + dot_nt(g_ref[2], w_ref[:, 2 * d :])
    n, root = normalized(x_ref[...].astype(f32))
    sums_ref[0:1, :] += jnp.sum(grad * n, axis=0, keepdims=True)
    sums_ref[1:2, :] += jnp.sum(grad, axis=0, keepdims=True)
    u = grad * gain_ref[...]
    u_mean = jnp.mean(u, axis=1, keepdims=True)
    un_mean = jnp.mean(u * n, axis=1, keepdims=True)
    gx_ref[...] = (gatt_ref[...].astype(f32) + root * (u - u_mean - n * un_mean)).astype(bf16)


def first_back(grad_qkv, weight, tokens, gatt, gain):
    rows, d = tokens.shape
    block = rows_of(ROW_BLOCK, d)
    return call(
        first_back_kernel,
        (rows // ROW_BLOCK,),
        [
            pl.BlockSpec((3, ROW_BLOCK, d), lambda i: (0, i, 0)),
            fixed((d, 3 * d)),
            block,
            block,
            fixed((1, d)),
        ],
        [block, kept((8, d))],
        [shape_of((rows, d), bf16), shape_of((8, d), f32)],
        micros=12,
        name="first_back",
    )(grad_qkv, weight, tokens, gatt, gain)


def dot_tn(a, b):
    return lax.dot_general(a, b, (((0,), (0,)), ((), ())), preferred_element_type=f32)


def expert_grad_kernel(
    up_owner_ref, down_owner_ref, arr_ref, gpre_ref, hidden_ref, garr_ref, up_ref, down_ref
):
    width = gpre_ref.shape[2]
    up = dot_tn(arr_ref[...], gpre_ref[0]).astype(bf16)
    for low in range(0, up.shape[0], width):
        up_ref[0, :, low : low + width] = up[low : low + width, :]
    down_ref[0] = dot_tn(hidden_ref[0], garr_ref[...]).astype(bf16)


def expert_grads(arriving, up_owners, down_owners, gpre, hidden, garr):
    _, rows, width = gpre.shape
    d = arriving.shape[1]
    m = up_owners.shape[0]
    return call(
        expert_grad_kernel,
        (m,),
        [
            fixed((rows, d)),
            pl.BlockSpec((1, rows, width), lambda t, up, down: (up[t], 0, 0)),
            pl.BlockSpec((1, rows, width), lambda t, up, down: (down[t], 0, 0)),
            fixed((rows, d)),
        ],
        [pl.BlockSpec((1, width, d), lambda t, *_: (t, 0, 0))] * 2,
        [shape_of((m, width, d), bf16)] * 2,
        prefetch=2,
        micros=7,
        name="expert_grads",
    )(up_owners, down_owners, arriving, gpre, hidden, garr)


def half_sums(terms):
    second = functools.reduce(lambda a, b: a + b, [ref[0].astype(f32) for ref in terms[1:]])
    return terms[0][0].astype(f32), second


def up_final_kernel(*refs):
    *terms, out_ref = refs
    width = terms[0].shape[2]
    for n, total in enumerate(half_sums(terms)):
        out_ref[:, n * width : (n + 1) * width] = total


def down_final_kernel(*refs):
    *terms, out_ref = refs
    for n, total in enumerate(half_sums(terms)):
        out_ref[n] = total


def up_final(*terms):
    _, width, d = terms[0].shape
    block = 128
    return call(
        up_final_kernel,
        (d // width, width // block),
        [pl.BlockSpec((1, block, width), lambda i, r: (0, r, i))] * len(terms),
        pl.BlockSpec((block, 2 * width), lambda i, r: (i * (width // block) + r, 0)),
        shape_of((d, 2 * width), f32),
        micros=1000,
        name="up_final",
    )(*terms)


def down_final(*terms):
    _, width, d = terms[0].shape
    block = 128
    return call(
        down_final_kernel,
        (width // block,),
        [pl.BlockSpec((1, block, d), lambda r: (0, r, 0))] * len(terms),
        pl.BlockSpec((2, block, d), lambda r: (0, r, 0)),
        shape_of((2, width, d), f32),
        micros=1000,
        name="down_final",
    )(*terms).reshape(2 * width, d)


def join_kernel(count, *refs):
    *terms, out_ref = refs
    left, right, lower = terms[:count], terms[count : 2 * count], terms[2 * count :]
    height, width = right[0].shape[2:]
    more = lower[0].shape[2]

    def total(parts):
        return functools.reduce(
            lambda a, b: a + b, [ref[0, 0].astype(f32) for ref in parts]
        ).astype(bf16)

    whole = total(left)
    out_ref[0, :height, :width] = whole[:height]
    out_ref[0, :height, width:] = total(right)
    out_ref[0, height : height + more, :] = total(lower)
    out_ref[0, height + more :, :width] = whole[height:]
    out_ref[0, height + more :, width:] = jnp.zeros_like(whole[height:])


def join(left, right, lower):
    levels, height, width = right.terms[0].shape[1:]
    more, rest = lower.terms[0].shape[2], left.terms[0].shape[2] - height
    if height % 16 or more % 16:
        left, right, lower = [part.finish(bf16) for part in (left, right, lower)]
        both = jnp.concatenate([left[:, :height], right], axis=2)
        last = jnp.pad(left[:, height:], ((0, 0), (0, 0), (0, width)))
        return jnp.concatenate([both, lower, last], axis=1)
    terms = left.terms + right.terms + lower.terms
    return Line.run(
        call(
            functools.partial(join_kernel, len(left.terms)),
            (levels,),
            [
                pl.BlockSpec((1, 1) + term.shape[2:], lambda z: (0, z, 0, 0)) for term in terms
            ],
            pl.BlockSpec((1, height + more + rest, 2 * width), lambda z: (z, 0, 0)),
            shape_of((levels, height + more + rest, 2 * width), bf16),
            micros=3,
            name="join",
        ),
        *terms,
    )


def swap(values, axis, bit):
    n = lax.axis_size(axis)
    return lax.ppermute(values, axis, [(i, i ^ bit) for i in range(n)])


def rows_kernel(sides, owner_ref, place_ref, ep_ref, a_ref, b_ref, *refs):
    *refs, grad_ref = refs
    extra_ref, out_refs = (refs[0], refs[1:]) if len(refs) % 2 else (None, refs)
    levels, height, width = out_refs[sides - 1].shape[1:]
    grad_ref[...] = dot_nn(a_ref[...], b_ref[...]).astype(bf16)
    for which in range(2):
        for z in range(levels):
            place = ep_ref[0] ^ (2 * reversed_bits(z, levels.bit_length() - 1) + 1 - which)
            rows = pl.ds(pl.multiple_of(place * height, height), height)
            for n in range(sides):
                out_refs[which * sides + n][0, z, :height, :] = grad_ref[
                    rows, n * width : (n + 1) * width
                ]
            if extra_ref is not None:
                out_refs[which * sides][0, z, height:, :] = extra_ref[0, place]


def rows_grad(a, b, owners, places, ep, copies, levels, sides, micros, extra=None):
    rows, d = b.shape
    height = a.shape[0] // (2 * copies * levels)
    width = d // sides
    if height % 16:
        away = [2 * reversed_bits(z, levels.bit_length() - 1) for z in range(levels)]

        def parts_of(values):
            values = jnp.take(values, owners, axis=0)
            return [
                jnp.take(values, ep[0] ^ (jnp.array(away, jnp.int32) + other), axis=1)
                for other in (1, 0)
            ]

        parts = parts_of(dot_nn(a, b).astype(bf16).reshape(copies, 2 * levels, height, d))
        result = [
            (part if n == 0 else jnp.take(part, places, axis=0))[
                ..., n * width : (n + 1) * width
            ]
            for part in parts
            for n in range(sides)
        ]
        if extra is not None:
            for which, rest in enumerate(parts_of(extra)):
                result[which * sides] = jnp.concatenate([result[which * sides], rest], axis=2)
        return result

    def shape(side):
        more = 0 if extra is None or side else extra.shape[2]
        return (levels, height + more, width)

    def piece(side):
        return pl.BlockSpec(
            (1,) + shape(side),
            lambda t, owner, place, ep: (place[t] if side else t, 0, 0, 0),
        )

    block = 2 * levels * height
    specs = [pl.BlockSpec((block, rows), lambda t, owner, *_: (owner[t], 0)), fixed((rows, d))]
    operands = [owners, places, ep, a, b]
    if extra is not None:
        specs.append(
            pl.BlockSpec((1,) + extra.shape[1:], lambda t, owner, *_: (owner[t], 0, 0, 0))
        )
        operands.append(extra)
    return call(
        functools.partial(rows_kernel, sides),
        (copies,),
        specs,
        [piece(side) for which in range(2) for side in range(sides)],
        [
            shape_of((copies,) + shape(side), bf16) for which in range(2) for side in range(sides)
        ],
        scratch=[pltpu.VMEM((block, d), bf16)],
        prefetch=3,
        micros=micros,
        name="rows_grad",
    )(*operands)


def add_kernel(*refs):
    *term_refs, out_ref = refs
    total = term_refs[0][...].astype(f32)
    for ref in term_refs[1:]:
        total = total + ref[...].astype(f32)
    out_ref[...] = total.astype(out_ref.dtype)


def add_terms(last, *others, first, count, kind):
    terms = [*others, last]
    shape = terms[0].shape
    columns = shape[-1]
    height = 1
    for extent in shape[1:-1]:
        height *= extent
    block = max(b for b in range(1, height + 1) if height % b == 0 and b * columns <= 1 << 18)
    result = call(
        add_kernel,
        (count, height // block),
        [pl.BlockSpec((1, block, columns), lambda t, r, *_: (first + t, r, 0)) for _ in terms],
        pl.BlockSpec((1, block, columns), lambda t, r, *_: (t, r, 0)),
        shape_of((count, height, columns), kind),
        micros=3,
        name="add_terms",
    )(*[term.reshape(term.shape[0], height, columns) for term in terms])
    return result.reshape((count,) + shape[1:])


class Halving:
    def __init__(self, terms, axis, bits, stride=1):
        self.terms, self.axis, self.bits, self.stride = terms, axis, list(bits), stride
        self.kind, self.extent = terms[0].dtype, 1 << len(self.bits)

    def add(self, first, kind):
        return Line.run(
            functools.partial(add_terms, first=first, count=self.extent, kind=kind),
            self.terms[-1], *self.terms[:-1],
        )

    def step(self, sent=None):
        if self.bits:
            if sent is None:
                self.extent //= 2
                sent = self.add(self.extent, self.kind)
            self.terms.append(swap(sent, self.axis, self.bits.pop(0) * self.stride))

    def finish(self, kind=f32):
        while self.bits:
            self.step()
        return self.add(0, kind)[0]


def reversed_bits(value, count):
    return sum(((value >> i) & 1) << (count - 1 - i) for i in range(count))


def shards(
    tokens, lengths, key_mask, routes, norm1_gain, norm1_bias, qkv_weight, out_weight,
    norm2_gain, norm2_bias, up_weight, down_weight, router_weight, mix_weight, expert_up,
    expert_down, cotangent,
):
    rows, d = tokens.shape
    groups, copies = lax.axis_size("ep"), lax.axis_size("dp")
    experts = expert_up.shape[0] * groups
    capacity = (5 * rows + 4 * experts - 1) // (4 * experts)
    slots = experts * capacity
    ep, dp = lax.axis_index("ep"), lax.axis_index("dp")
    core, level, levels = ep % 2, ep // 2, groups // 2
    count = copies.bit_length() - 1
    up_bits = [1 << i for i in reversed(range(count))]
    down_bits = [1 << i for i in range(count)]
    level_bits = [1 << i for i in range(levels.bit_length() - 1)]
    level_groups = [[2 * z + c for z in range(levels)] for c in range(2)]
    order = jnp.arange(copies, dtype=jnp.int32)
    back_order = jnp.array([reversed_bits(t, count) for t in range(copies)], jnp.int32)
    owners = dp.astype(jnp.int32) ^ order
    back_owners = dp.astype(jnp.int32) ^ back_order
    core_scalar = core.astype(jnp.int32).reshape(1)
    ep_scalar = ep.astype(jnp.int32).reshape(1)

    row_at = jnp.arange(rows, dtype=jnp.int32)
    live = row_at < lengths[0]
    flat_routes = routes[:, 0]
    routed = (flat_routes[:, None] == jnp.arange(experts)[None, :]) & live[:, None]
    ahead = dot_nn(
        (row_at[None, :] < row_at[:, None]).astype(bf16), routed.astype(bf16)
    )
    place = jnp.sum(jnp.where(routed, ahead, 0.0), axis=1).astype(jnp.int32)
    target = jnp.where(live, flat_routes * capacity + place, slots)
    target_column = target[:, None]
    pick = (jnp.arange(slots, dtype=jnp.int32)[:, None] == target[None, :]).astype(bf16)

    def exchange(values):
        return lax.all_to_all(
            values.reshape(groups, slots // groups, d), "ep", 0, 0, tiled=True
        ).reshape(slots, d)

    def sort_rows(values):
        return dot_nn(pick, values).astype(bf16)

    run = Line.run
    Line.last = None
    cot_arriving = exchange(run(sort_rows, cotangent))
    usable = live & (key_mask == 1)
    bias = jnp.where(usable, 0.0, MASKED).astype(f32)[:, None]
    mix_padded = jnp.pad(mix_weight, ((0, 0), (0, LANES - 2)))
    gate_padded = jnp.pad(
        jnp.concatenate([router_weight, mix_weight], axis=1),
        ((0, 0), (0, LANES - 2 - experts)),
    )
    first, qkv = run(ln_qkv, tokens, norm1_gain[None], norm1_bias[None], qkv_weight)
    context, context_t, lse = run(attend, qkv, bias)
    middle, second, second_t, gdl, gdl_t, mixing = run(
        after, tokens, core_scalar, context, cotangent, out_weight, norm2_gain[None],
        norm2_bias[None], mix_padded, d // groups,
    )
    cot_arriving, second = lax.optimization_barrier((cot_arriving, second))
    arriving = exchange(run(sort_rows, second))

    orders = (owners, up_bits), (back_owners, down_bits)
    parts = [
        run(dense, second, chunk, order, levels, second_t, gdl, gdl_t, up_weight, down_weight)
        for chunk, (order, _) in enumerate(orders)
    ]
    sums, lower = [], []
    half = copies // 2
    for (_, _, keep, send, keep_next, send_next), (_, bits) in zip(parts, orders):
        got_next, got = swap(send_next, "ep", 1), swap(send, "ep", 1)
        lower.append(got)
        sums.append(Halving([keep, got], "dp", bits))
        sums[-1].extent = half
        sums[-1].step(
            run(
                functools.partial(add_terms, first=0, count=half, kind=bf16), got_next, keep_next
            )
        )
    Line.others = tuple(lower)
    given = copies, ep_scalar, cot_arriving, gate_padded, expert_up[0], expert_down[0], experts
    m = copies // 2

    def expert_part(first, gpre, hidden):
        at = slice(m, None) if first else slice(0, m)
        return run(expert_grads, arriving, owners[at], back_owners[at], gpre, hidden, garr)

    def swapped(pair):
        return [swap(sent, "dp", bits[0]) for sent, bits in zip(pair, (up_bits, down_bits))]

    hidden0, gpre0, garr, *before = run(expert, arriving, 0, *given)
    got0 = swapped(expert_part(True, gpre0, hidden0))
    hidden1, gpre1, sent, gin, gate_grad = run(expert, arriving, 1, *given, [garr, *before])
    grad_back = exchange(gin)
    dense_out, grad_second = run(
        dense_rest, parts[0][0], owners, back_order, parts[1][0], parts[0][1], parts[1][1], up_weight,
        down_weight,
    )
    for side in sums:
        side.step()
    got1 = swapped(expert_part(True, gpre1, hidden1))

    def halvings(keeps, gots):
        return [
            Halving([keep, got], "dp", bits[1:])
            for keep, got, bits in zip(keeps, gots, (up_bits, down_bits))
        ]

    halves0 = halvings(expert_part(False, gpre0, hidden0), got0)
    for side in halves0:
        side.step()
    pieces = [
        lax.psum_scatter(
            side.finish(bf16), "ep", scatter_dimension=0, axis_index_groups=level_groups
        )
        for side in sums
    ]
    halves1 = halvings(expert_part(False, gpre1, hidden1), got1)
    gatt, grad_context, sums2 = run(
        between, grad_second, target_column, grad_back, dense_out, middle, mixing, cotangent,
        second, mix_weight.T.astype(f32), norm2_gain[None], out_weight,
    )

    sent, gatt = lax.optimization_barrier((sent, gatt))
    expert_back = exchange(sent)

    def own_rows(a, b, all_bits, micros, extra=None):
        sides = len(all_bits)
        result = run(
            rows_grad, a, b, owners, back_order, ep_scalar, copies, levels, sides, micros,
            extra,
        )
        return [
            Halving([keep, swap(send, "ep", 1)], "dp", bits)
            for send, keep, bits in zip(result[:sides], result[sides:], all_bits)
        ]

    (out_side,) = own_rows(context_t, gatt, [up_bits], 3)
    grad_qkv, grad_qkv_t = run(attend_back, qkv, bias, lse, grad_context)
    done0 = [side.finish(bf16)[None] for side in halves0]
    for side in halves1:
        side.step()
    grad_inputs, sums1 = run(first_back, grad_qkv, qkv_weight, tokens, gatt, norm1_gain[None])
    home_mix = jnp.concatenate(
        [jnp.zeros((experts, d), f32), sums2[2:3], -sums2[2:3]], axis=0
    )
    small = jnp.concatenate(
        [sums1[:2], sums2[:2], gate_grad[: experts + 2] + home_mix], axis=0
    )
    kinds = small.shape[0]
    small = small.reshape(kinds, copies, groups, -1).transpose(1, 2, 0, 3)
    own = small.shape[3]
    small = small.reshape(copies, groups, 1, kinds * own).astype(bf16)
    small = jnp.pad(small, ((0, 0), (0, 0), (0, 15), (0, d // 2 - kinds * own)))
    qkv_sides = own_rows(
        grad_qkv_t.reshape(3 * d, rows), first, [up_bits, down_bits], 7, small
    )
    expert_up_sum, expert_down_sum = [
        run(final, first_half, *second_half.terms)
        for final, first_half, second_half in zip((up_final, down_final), done0, halves1)
    ]
    for side in qkv_sides:
        side.step()
    out_side.step()
    outputs = run(outputs_of, dense_out, target_column, expert_back, middle, mixing)
    for side in qkv_sides:
        side.step()
    out_side.step()
    whole = Halving([join(*qkv_sides, out_side)], "ep", level_bits, 2).finish()
    height = 3 * d // (copies * groups)
    qkv_sum, out_sum = whole[:height].T, whole[height : height + own]
    small = whole[height + own, : kinds * own].reshape(kinds, own).T
    pieces = [piece.astype(f32) for piece in pieces]
    up_sum, down_sum = [jnp.concatenate([piece[n] for piece in pieces], axis=1) for n in range(2)]
    down_sum = down_sum.T
    Line.last = None
    return (
        outputs, grad_inputs, small[:, 0], small[:, 1], qkv_sum, out_sum, small[:, 2],
        small[:, 3], up_sum, down_sum, small[:, 4 : 4 + experts], small[:, 4 + experts :],
        expert_up_sum[None], expert_down_sum[None],
    )


def solution(mesh):
    split = ("dp", "ep")
    return jax.shard_map(
        shards,
        mesh=mesh,
        in_specs=(
            P(split, None), P(split), P(split), P(split, None), P(), P(), P(), P(), P(), P(),
            P(), P(), P(), P(), P("ep", None, None), P("ep", None, None), P(split, None),
        ),
        out_specs=(
            P(split, None), P(split, None), P(split), P(split), P(None, split), P(split, None),
            P(split), P(split), P("ep", "dp"), P("dp", "ep"), P(split, None), P(split, None),
            P("ep", None, "dp"), P("ep", "dp", None),
        ),
        check_vma=False,
    )
```

```python
import functools

import jax
import jax.numpy as jnp
from jax import lax
from jax.experimental import pallas as pl
from jax.experimental.pallas import tpu as pltpu
from jax.sharding import PartitionSpec as P

HEAD_DIM = 64
EPSILON = 1e-05
MASKED = -1e30
ROW_BLOCK = 256
CHUNKS = 2
WEIGHT = 0.01
EXPERT_PARTS = 1
DENSE_BLOCK = 256
LANES = 128
GELU_ROOT = 0.7978845608028654
GELU_CUBE = 0.044715
LOG2_E = 1.4426950408889634

f32 = jnp.float32
bf16 = jnp.bfloat16


def dot_nn(a, b):
    return lax.dot_general(a, b, (((1,), (0,)), ((), ())), preferred_element_type=f32)


def dot_nt(a, b):
    return lax.dot_general(a, b, (((1,), (1,)), ((), ())), preferred_element_type=f32)


class Line:
    last = None
    others = ()

    @classmethod
    def run(cls, function, *values):
        result = function(*values)
        cls.last = jax.tree.leaves(result)[0]
        return result


def call(kernel, grid, in_specs, out_specs, out_shape, micros, scratch=(), prefetch=0, name=None):
    def apply(*operands):
        specs, count, ordered = list(in_specs), len(operands), kernel
        if Line.last is not None:
            unread = (Line.last,) + Line.others
            Line.others = ()
            specs += [pl.BlockSpec(memory_space=pl.ANY)] * len(unread)
            operands += unread

            def ordered(*refs):
                kernel(*refs[:count], *refs[count + len(unread) :])

        return pl.pallas_call(
            ordered,
            grid_spec=pltpu.PrefetchScalarGridSpec(
                num_scalar_prefetch=prefetch,
                grid=grid,
                in_specs=specs,
                out_specs=out_specs,
                scratch_shapes=list(scratch),
            ),
            out_shape=out_shape,
            compiler_params=pltpu.CompilerParams(
                dimension_semantics=("arbitrary",) * len(grid), vmem_limit_bytes=63 * 1024 * 1024
            ),
            cost_estimate=pl.CostEstimate(
                flops=int(micros * WEIGHT * 1.15e9),
                bytes_accessed=int(micros * WEIGHT * 3e6),
                transcendentals=0,
            ),
            name=name,
        )(*operands)

    return apply


def fixed(shape):
    return pl.BlockSpec(
        shape, lambda *_: (0,) * len(shape), pipeline_mode=pl.Buffered(buffer_count=1)
    )


def kept(shape):
    return pl.BlockSpec(shape, lambda *_: (0,) * len(shape))


def rows_of(height, width):
    return pl.BlockSpec((height, width), lambda i, *_: (i, 0))


def shape_of(shape, dtype):
    return jax.ShapeDtypeStruct(shape, dtype)


def normalized(values):
    average = jnp.mean(values, axis=1, keepdims=True)
    centered = values - average
    root = lax.rsqrt(jnp.mean(centered * centered, axis=1, keepdims=True) + EPSILON)
    return centered * root, root


def gelu_pair(v):
    square = v * v
    t = jnp.tanh(v * (GELU_ROOT + (GELU_ROOT * GELU_CUBE) * square))
    half = 0.5 + 0.5 * t
    slope = half + (v * (0.5 - 0.5 * (t * t))) * (
        GELU_ROOT + (3.0 * GELU_ROOT * GELU_CUBE) * square
    )
    return v * half, slope


def ln_qkv_kernel(x_ref, g_ref, b_ref, w_ref, first_ref, qkv_ref):
    @pl.when(pl.program_id(0) == 0)
    def _():
        def some_rows(i, carry):
            at = pl.ds(pl.multiple_of(i * LANES, LANES), LANES)
            n, _ = normalized(x_ref[at, :].astype(f32))
            first_ref[at, :] = (n * g_ref[...] + b_ref[...]).astype(bf16)
            return carry

        lax.fori_loop(0, x_ref.shape[0] // LANES, some_rows, 0)

    qkv_ref[...] = dot_nn(first_ref[...], w_ref[...]).astype(bf16)


def ln_qkv(tokens, gain, bias, weight):
    rows, d = tokens.shape
    width = weight.shape[1]
    block = 1024
    return call(
        ln_qkv_kernel,
        (width // block,),
        [
            fixed((rows, d)),
            fixed((1, d)),
            fixed((1, d)),
            pl.BlockSpec((d, block), lambda i: (0, i)),
        ],
        [kept((rows, d)), pl.BlockSpec((rows, block), lambda i: (0, i))],
        [shape_of((rows, d), bf16), shape_of((rows, width), bf16)],
        micros=11,
        name="ln_qkv",
    )(tokens, gain, bias, weight)


def diagonal_bias(bias_rows):
    size = bias_rows.shape[0]
    key_at = lax.broadcasted_iota(jnp.int32, (size, size), 0)
    query_at = lax.broadcasted_iota(jnp.int32, (size, size), 1)
    return jnp.where(
        key_at == query_at, 0.0, jnp.where(key_at < query_at, bias_rows, MASKED)
    )


def head_lanes(values, head):
    lane = lax.broadcasted_iota(jnp.int32, values.shape, 1)
    inside = (lane >= head * HEAD_DIM) & (lane < (head + 1) * HEAD_DIM)
    return jnp.where(inside, values, jnp.zeros_like(values))


def attend_kernel(bias_ref, q_ref, k_ref, v_ref, ctx_ref, ctx_t_ref, lse_ref):
    rows = q_ref.shape[0]
    v_t = v_ref[...].T
    for i in range(rows // ROW_BLOCK):
        low, high = i * ROW_BLOCK, (i + 1) * ROW_BLOCK
        edge = diagonal_bias(bias_ref[low:high, :])
        q = (q_ref[low:high, :].astype(f32) * (HEAD_DIM**-0.5 * LOG2_E)).astype(bf16)
        sides = []
        for head in range(2):
            q_head = head_lanes(q, head)
            inner = dot_nt(k_ref[low:high, :], q_head) + edge
            top = jnp.max(inner, axis=0, keepdims=True)
            if i:
                outer = dot_nt(k_ref[:low, :], q_head) + bias_ref[:low, :]
                top = jnp.maximum(top, jnp.max(outer, axis=0, keepdims=True))
            inner = jnp.exp2(inner - top)
            total = jnp.sum(inner, axis=0, keepdims=True)
            v_head = v_t[head * HEAD_DIM : (head + 1) * HEAD_DIM, :]
            side = dot_nn(v_head[:, low:high], inner.astype(bf16))
            if i:
                outer = jnp.exp2(outer - top)
                total = total + jnp.sum(outer, axis=0, keepdims=True)
                side = side + dot_nn(v_head[:, :low], outer.astype(bf16))
            sides.append(side / total)
            lse_ref[0, head : head + 1, low:high] = top + jnp.log2(total)
        both = jnp.concatenate(sides, axis=0)
        ctx_t_ref[:, low:high] = both.astype(bf16)
        ctx_ref[low:high, :] = both.T.astype(bf16)


def attend(qkv, bias):
    rows, d = qkv.shape[0], qkv.shape[1] // 3
    pairs = d // LANES

    def third(n):
        return pl.BlockSpec((rows, LANES), lambda h: (0, n * pairs + h))

    return call(
        attend_kernel,
        (pairs,),
        [fixed((rows, 1)), third(0), third(1), third(2)],
        [
            third(0),
            pl.BlockSpec((LANES, rows), lambda h: (h, 0)),
            pl.BlockSpec((1, 8, rows), lambda h: (h, 0, 0)),
        ],
        [
            shape_of((rows, d), bf16),
            shape_of((d, rows), bf16),
            shape_of((pairs, 8, rows), f32),
        ],
        micros=22,
        name="attend",
    )(bias, qkv, qkv, qkv)


def attend_back_kernel(
    bias_ref, lse_ref, q_ref, k_ref, v_ref, do_ref, g_ref, g_t_ref, gk_acc, gv_acc
):
    rows = q_ref.shape[0]
    scale = HEAD_DIM**-0.5
    k_t = k_ref[...].T
    gk_acc[...] = jnp.zeros_like(gk_acc)
    gv_acc[...] = jnp.zeros_like(gv_acc)
    for i in range(rows // ROW_BLOCK):
        low, high = i * ROW_BLOCK, (i + 1) * ROW_BLOCK
        edge = diagonal_bias(bias_ref[low:high, :])
        q = q_ref[low:high, :] * jnp.asarray(scale, bf16)
        raised = (q_ref[low:high, :].astype(f32) * (scale * LOG2_E)).astype(bf16)
        do = do_ref[low:high, :]
        sides = []
        for head in range(2):
            q_head = head_lanes(q, head)
            raised_head = head_lanes(raised, head)
            do_head = head_lanes(do, head)
            lse = lse_ref[0, head : head + 1, low:high]
            spans = [(low, high, edge)]
            if i:
                spans.append((0, low, bias_ref[:low, :]))
            probs, grads = [], []
            dots = 0.0
            for start, stop, bias in spans:
                p = jnp.exp2(dot_nt(k_ref[start:stop, :], raised_head) + bias - lse)
                gp = dot_nt(v_ref[start:stop, :], do_head)
                dots = dots + jnp.sum(p * gp, axis=0, keepdims=True)
                probs.append(p)
                grads.append(gp)
            side = 0.0
            k_head = k_t[head * HEAD_DIM : (head + 1) * HEAD_DIM, :]
            for (start, stop, _), p, gp in zip(spans, probs, grads):
                ds = (p * (gp - dots)).astype(bf16)
                gv_acc[start:stop, :] += dot_nn(p.astype(bf16), do_head)
                gk_acc[start:stop, :] += dot_nn(ds, q_head)
                side = side + dot_nn(k_head[:, start:stop], ds)
            sides.append(side * scale)
        both = jnp.concatenate(sides, axis=0)
        g_t_ref[0, :, low:high] = both.astype(bf16)
        g_ref[0, low:high, :] = both.T.astype(bf16)
    for n, acc in ((1, gk_acc), (2, gv_acc)):
        g_ref[n] = acc[...].astype(bf16)
        g_t_ref[n] = acc[...].T.astype(bf16)


def attend_back(qkv, bias, lse, grad_context):
    rows, d = grad_context.shape
    pairs = d // LANES

    def third(n):
        return pl.BlockSpec((rows, LANES), lambda h: (0, n * pairs + h))

    return call(
        attend_back_kernel,
        (pairs,),
        [
            fixed((rows, 1)),
            pl.BlockSpec((1, 8, rows), lambda h: (h, 0, 0)),
            third(0),
            third(1),
            third(2),
            third(0),
        ],
        [
            pl.BlockSpec((3, rows, LANES), lambda h: (0, 0, h)),
            pl.BlockSpec((3, LANES, rows), lambda h: (0, h, 0)),
        ],
        [shape_of((3, rows, d), bf16), shape_of((3, d, rows), bf16)],
        scratch=[pltpu.VMEM((rows, LANES), f32), pltpu.VMEM((rows, LANES), f32)],
        micros=28,
        name="attend_back",
    )(bias, lse, qkv, qkv, qkv, grad_context)


def after_kernel(
    rb, core_ref, x_ref, ctx_ref, cot_ref, w_ref, g_ref, b_ref, mix_ref,
    middle_ref, second_ref, second_t_ref, gdl_ref, gdl_t_ref, mixing_ref,
):
    d = x_ref.shape[1]
    middle = x_ref[...].astype(f32) + dot_nn(ctx_ref[...], w_ref[...])
    middle_ref[...] = middle
    n, _ = normalized(middle)
    second = (n * g_ref[...] + b_ref[...]).astype(bf16)
    second_ref[...] = second
    logits = dot_nn(second, mix_ref[...])
    gap = logits[:, 1:2] - logits[:, 0:1]
    first_share = 1.0 / (1.0 + jnp.exp(gap))
    other_share = 1.0 / (1.0 + jnp.exp(-gap))
    lane = lax.broadcasted_iota(jnp.int32, mixing_ref.shape, 1)
    mixing_ref[...] = jnp.where(lane == 0, first_share, other_share)
    gdl = (first_share * cot_ref[...].astype(f32)).astype(bf16)
    gdl_ref[...] = gdl
    core = core_ref[0]
    for values, target in ((second, second_t_ref), (gdl, gdl_t_ref)):
        turned = values.astype(f32).T.astype(bf16)
        for piece in range(d // rb):
            place = ((piece % 2) ^ core) * (d // (2 * rb)) + piece // 2
            target[pl.ds(pl.multiple_of(place * rb, rb), rb), :] = turned[
                piece * rb : (piece + 1) * rb, :
            ]


def after(tokens, core, context, cotangent, weight, gain, bias, mix_padded, rb):
    rows, d = tokens.shape
    block = rows_of(ROW_BLOCK, d)
    turned = pl.BlockSpec((d, ROW_BLOCK), lambda i, *_: (0, i))
    return call(
        functools.partial(after_kernel, rb),
        (rows // ROW_BLOCK,),
        [block, block, block, fixed((d, d)), fixed((1, d)), fixed((1, d)), fixed((d, LANES))],
        [block, block, turned, block, turned, rows_of(ROW_BLOCK, LANES)],
        [
            shape_of((rows, d), f32),
            shape_of((rows, d), bf16),
            shape_of((d, rows), bf16),
            shape_of((rows, d), bf16),
            shape_of((d, rows), bf16),
            shape_of((rows, LANES), f32),
        ],
        prefetch=1,
        micros=10,
        name="after",
    )(core, tokens, context, cotangent, weight, gain, bias, mix_padded)


def dense_kernel(
    owner_ref, second_ref, second_t_ref, gdl_ref, gdl_t_ref, up_ref, down_ref,
    hidden_ref, gpre_ref, keep_ref, send_ref, keep_next_ref, send_next_ref,
):
    rows = second_ref.shape[0]
    half = second_t_ref.shape[0] // 2
    levels = keep_ref.shape[1]
    for low in range(0, rows, DENSE_BLOCK):
        at = slice(low, low + DENSE_BLOCK)
        value, slope = gelu_pair(dot_nn(second_ref[at, :], up_ref[...]))
        hidden_ref[0, at, :] = value.astype(bf16)
        gpre_ref[0, at, :] = (dot_nt(gdl_ref[at, :], down_ref[...]) * slope).astype(bf16)

    def write(keep, send):
        for n, lhs_ref, units_ref in ((0, second_t_ref, gpre_ref), (1, gdl_t_ref, hidden_ref)):
            for target, low in ((keep, 0), (send, half)):
                grad = dot_nn(lhs_ref[low : low + half, :], units_ref[0]).astype(bf16)
                for z in range(levels):
                    target[0, z, n] = grad[z * (half // levels) : (z + 1) * (half // levels)]

    upper = pl.program_id(0) >= pl.num_programs(0) // 2
    pl.when(jnp.logical_not(upper))(lambda: write(keep_ref, send_ref))
    pl.when(upper)(lambda: write(keep_next_ref, send_next_ref))


def dense(second, chunk, owners, levels, second_t, gdl, gdl_t, up, down):
    rows, d = second.shape
    n = owners.shape[0]
    width = up.shape[1] // (n * CHUNKS)
    shape = (levels, 2, d // (2 * levels), width)
    lower = pl.BlockSpec((1,) + shape, lambda t, _: (jnp.minimum(t, n // 2 - 1), 0, 0, 0, 0))
    upper = pl.BlockSpec((1,) + shape, lambda t, _: (jnp.maximum(t - n // 2, 0), 0, 0, 0, 0))
    units = pl.BlockSpec((1, rows, width), lambda t, _: (t, 0, 0))
    return call(
        dense_kernel,
        (n,),
        [
            fixed((rows, d)),
            fixed((d, rows)),
            fixed((rows, d)),
            fixed((d, rows)),
            pl.BlockSpec((d, width), lambda t, owner: (0, owner[t] * CHUNKS + chunk)),
            pl.BlockSpec((width, d), lambda t, owner: (owner[t] * CHUNKS + chunk, 0)),
        ],
        [units, units, lower, lower, upper, upper],
        [shape_of((n, rows, width), bf16)] * 2
        + [shape_of((n // 2,) + shape, bf16)] * 4,
        prefetch=1,
        micros=100,
        name="dense",
    )(owners, second, second_t, gdl, gdl_t, up, down)


def dense_rest_kernel(
    owner_ref, place_ref, hidden0_ref, hidden1_ref, gpre0_ref, gpre1_ref, up_ref, down_ref,
    out_ref, gsec_ref,
):
    width = hidden0_ref.shape[2]

    @pl.when(pl.program_id(0) == 0)
    def _():
        out_ref[...] = jnp.zeros_like(out_ref)
        gsec_ref[...] = jnp.zeros_like(gsec_ref)

    out_ref[...] += dot_nn(hidden0_ref[0], down_ref[:width, :]) + dot_nn(
        hidden1_ref[0], down_ref[width:, :]
    )
    gsec_ref[...] += dot_nt(gpre0_ref[0], up_ref[:, :width]) + dot_nt(
        gpre1_ref[0], up_ref[:, width:]
    )


def dense_rest(hidden0, owners, places, hidden1, gpre0, gpre1, up, down):
    n, rows, width = hidden0.shape
    d = up.shape[0]
    units0 = pl.BlockSpec((1, rows, width), lambda t, owner, place: (t, 0, 0))
    units1 = pl.BlockSpec((1, rows, width), lambda t, owner, place: (place[t], 0, 0))
    return call(
        dense_rest_kernel,
        (n,),
        [
            units0,
            units1,
            units0,
            units1,
            pl.BlockSpec((d, 2 * width), lambda t, owner, _: (0, owner[t])),
            pl.BlockSpec((2 * width, d), lambda t, owner, _: (owner[t], 0)),
        ],
        [kept((rows, d))] * 2,
        [shape_of((rows, d), f32)] * 2,
        prefetch=2,
        micros=3000,
        name="dense_rest",
    )(owners, places, hidden0, hidden1, gpre0, gpre1, up, down)


def shares(logits, experts, me):
    lane = lax.broadcasted_iota(jnp.int32, logits.shape, 1)

    def softmax(inside):
        held = jnp.where(inside, logits, MASKED)
        raised = jnp.where(inside, jnp.exp(held - jnp.max(held, axis=1, keepdims=True)), 0.0)
        return raised / jnp.sum(raised, axis=1, keepdims=True)

    def pick(values, at):
        return jnp.sum(jnp.where(lane == at, values, 0.0), axis=1, keepdims=True)

    gates = softmax(lane < experts)
    mixing = softmax((lane >= experts) & (lane < experts + 2))
    return gates, pick(gates, me), pick(mixing, experts), pick(mixing, experts + 1)


def expert_step(arr_ref, garr_ref, up_ref, down_ref, hidden_ref, gpre_ref, out_acc, gin_acc):
    rows = arr_ref.shape[0]
    step = rows // EXPERT_PARTS
    for low in range(0, rows, step):
        at = slice(low, low + step)
        value, slope = gelu_pair(dot_nn(arr_ref[at, :], up_ref[...]))
        h = value.astype(bf16)
        g = (dot_nt(garr_ref[at, :], down_ref[...]) * slope).astype(bf16)
        gpre_ref[0, at, :] = g
        out_acc[at, :] += dot_nn(h, down_ref[...])
        gin_acc[at, :] += dot_nt(g, up_ref[...])
        hidden_ref[0, at, :] = h


def expert_first_kernel(
    experts, me_ref, arr_ref, cot_ref, gate_ref, up_ref, down_ref,
    hidden_ref, gpre_ref, garr_ref, logit_ref, out_acc, gin_acc,
):
    rows = arr_ref.shape[0]
    step = rows // EXPERT_PARTS

    @pl.when(pl.program_id(0) == 0)
    def _():
        out_acc[...] = jnp.zeros_like(out_acc)
        gin_acc[...] = jnp.zeros_like(gin_acc)
        for low in range(0, rows, step):
            at = slice(low, low + step)
            logits = dot_nn(arr_ref[at, :], gate_ref[...])
            logit_ref[at, :] = logits
            _, chosen, _, mix1 = shares(logits, experts, me_ref[0])
            garr_ref[at, :] = ((chosen * mix1) * cot_ref[at, :].astype(f32)).astype(bf16)

    expert_step(arr_ref, garr_ref, up_ref, down_ref, hidden_ref, gpre_ref, out_acc, gin_acc)


def expert_second_kernel(
    experts, me_ref, arr_ref, cot_ref, gate_ref, up_ref, down_ref, garr_ref, logit_ref, out_ref,
    grad_ref, hidden_ref, gpre_ref, sent_ref, gin_ref, gate_grad_ref, out_acc, gin_acc,
):
    rows = arr_ref.shape[0]
    step = rows // EXPERT_PARTS
    me = me_ref[0]

    @pl.when(pl.program_id(0) == 0)
    def _():
        out_acc[...] = out_ref[...]
        gin_acc[...] = grad_ref[...]

    expert_step(arr_ref, garr_ref, up_ref, down_ref, hidden_ref, gpre_ref, out_acc, gin_acc)

    @pl.when(pl.program_id(0) == pl.num_programs(0) - 1)
    def _():
        gate_grad = 0.0
        lane = lax.broadcasted_iota(jnp.int32, (step, LANES), 1)
        for low in range(0, rows, step):
            at = slice(low, low + step)
            gates, chosen, mix0, mix1 = shares(logit_ref[at, :], experts, me)
            out = out_acc[at, :]
            sent_ref[at, :] = ((chosen * mix1) * out).astype(bf16)
            met = jnp.sum(cot_ref[at, :].astype(f32) * out, axis=1, keepdims=True)
            grad_chosen = mix1 * met
            swing = chosen * met * mix0 * mix1
            grad = gates * grad_chosen * (jnp.where(lane == me, 1.0, 0.0) - chosen)
            grad = grad + jnp.where(lane == experts + 1, swing, 0.0)
            grad = grad - jnp.where(lane == experts, swing, 0.0)
            low_grad = grad.astype(bf16)
            gin_ref[at, :] = (gin_acc[at, :] + dot_nt(low_grad, gate_ref[...])).astype(bf16)
            gate_grad = gate_grad + dot_nn(grad.T.astype(bf16), arr_ref[at, :])
        gate_grad_ref[...] = gate_grad


def expert(arriving, half, n, me, cot, gate_padded, up, down, experts, before=None):
    rows, d = arriving.shape
    width = up.shape[1] // (2 * n)
    units = pl.BlockSpec((1, rows, width), lambda t, *_: (t, 0, 0))
    specs = [
        fixed((rows, d)),
        fixed((rows, d)),
        fixed((d, LANES)),
        pl.BlockSpec((d, width), lambda t, *_: (0, 2 * t + half)),
        pl.BlockSpec((width, d), lambda t, *_: (2 * t + half, 0)),
    ]
    shapes = [shape_of((n, rows, width), bf16)] * 2
    if half == 0:
        return call(
            functools.partial(expert_first_kernel, experts),
            (n,),
            specs,
            [units, units] + [kept((rows, d)), kept((rows, LANES))] + [kept((rows, d))] * 2,
            shapes
            + [shape_of((rows, d), bf16), shape_of((rows, LANES), f32)]
            + [shape_of((rows, d), f32)] * 2,
            prefetch=1,
            micros=4800,
            name="expert_first",
        )(me, arriving, cot, gate_padded, up, down)
    return call(
        functools.partial(expert_second_kernel, experts),
        (n,),
        specs + [fixed((rows, d)), fixed((rows, LANES)), fixed((rows, d)), fixed((rows, d))],
        [units, units] + [kept((rows, d))] * 2 + [kept((LANES, d))],
        shapes + [shape_of((rows, d), bf16)] * 2 + [shape_of((LANES, d), f32)],
        scratch=[pltpu.VMEM((rows, d), f32), pltpu.VMEM((rows, d), f32)],
        prefetch=1,
        micros=100,
        name="expert_second",
    )(me, arriving, cot, gate_padded, up, down, *before)


def between_kernel(
    target_ref, gin_ref, gs_ref, do_ref, middle_ref, mixing_ref, cot_ref,
    second_ref, mix_t_ref, g_ref, w_ref, gatt_ref, gctx_ref, sums_ref,
):
    @pl.when(pl.program_id(0) == 0)
    def _():
        sums_ref[...] = jnp.zeros_like(sums_ref)

    slots = gin_ref.shape[0]
    lane = lax.broadcasted_iota(jnp.int32, (ROW_BLOCK, slots), 1)
    pick = jnp.where(target_ref[...] == lane, 1.0, 0.0).astype(bf16)
    grad = gs_ref[...] + dot_nn(pick, gin_ref[...])
    go = cot_ref[...].astype(f32)
    met = jnp.sum(go * do_ref[...], axis=1, keepdims=True)
    swing = met * mixing_ref[:, 0:1] * mixing_ref[:, 1:2]
    grad = grad + swing * (mix_t_ref[0:1, :] - mix_t_ref[1:2, :])
    n, root = normalized(middle_ref[...])
    sums_ref[0:1, :] += jnp.sum(grad * n, axis=0, keepdims=True)
    sums_ref[1:2, :] += jnp.sum(grad, axis=0, keepdims=True)
    sums_ref[2:3, :] += jnp.sum(second_ref[...].astype(f32) * swing, axis=0, keepdims=True)
    u = grad * g_ref[...]
    u_mean = jnp.mean(u, axis=1, keepdims=True)
    un_mean = jnp.mean(u * n, axis=1, keepdims=True)
    gatt = (go + root * (u - u_mean - n * un_mean)).astype(bf16)
    gatt_ref[...] = gatt
    gctx_ref[...] = dot_nt(gatt, w_ref[...]).astype(bf16)


def between(gs, target, gin, do, middle, mixing, cotangent, second, mix_t, gain, weight):
    rows, d = middle.shape
    slots = gin.shape[0]
    block = rows_of(ROW_BLOCK, d)
    return call(
        between_kernel,
        (rows // ROW_BLOCK,),
        [
            rows_of(ROW_BLOCK, 1), fixed((slots, d)), block, block, block,
            rows_of(ROW_BLOCK, LANES), block, block, fixed((2, d)), fixed((1, d)), fixed((d, d)),
        ],
        [block, block, kept((8, d))],
        [shape_of((rows, d), bf16), shape_of((rows, d), bf16), shape_of((8, d), f32)],
        micros=12,
        name="between",
    )(
        target, gin, gs, do, middle, mixing, cotangent, second, mix_t, gain,
        weight,
    )


def out_kernel(target_ref, back_ref, do_ref, middle_ref, mixing_ref, out_ref):
    slots = back_ref.shape[0]
    lane = lax.broadcasted_iota(jnp.int32, (ROW_BLOCK, slots), 1)
    pick = jnp.where(target_ref[...] == lane, 1.0, 0.0).astype(bf16)
    mixed = mixing_ref[:, 0:1] * do_ref[...] + dot_nn(pick, back_ref[...])
    out_ref[...] = (middle_ref[...] + mixed).astype(bf16)


def outputs_of(do, target, back, middle, mixing):
    rows, d = middle.shape
    slots = back.shape[0]
    block = rows_of(ROW_BLOCK, d)
    return call(
        out_kernel,
        (rows // ROW_BLOCK,),
        [
            rows_of(ROW_BLOCK, 1), fixed((slots, d)), block, block,
            rows_of(ROW_BLOCK, LANES),
        ],
        block,
        shape_of((rows, d), bf16),
        micros=1000,
        name="outputs",
    )(target, back, do, middle, mixing)


def first_back_kernel(g_ref, w_ref, x_ref, gatt_ref, gain_ref, gx_ref, sums_ref):
    d = x_ref.shape[1]

    @pl.when(pl.program_id(0) == 0)
    def _():
        sums_ref[...] = jnp.zeros_like(sums_ref)

    grad = dot_nt(g_ref[0], w_ref[:, :d])
    grad = grad + dot_nt(g_ref[1], w_ref[:, d : 2 * d])
    grad = grad + dot_nt(g_ref[2], w_ref[:, 2 * d :])
    n, root = normalized(x_ref[...].astype(f32))
    sums_ref[0:1, :] += jnp.sum(grad * n, axis=0, keepdims=True)
    sums_ref[1:2, :] += jnp.sum(grad, axis=0, keepdims=True)
    u = grad * gain_ref[...]
    u_mean = jnp.mean(u, axis=1, keepdims=True)
    un_mean = jnp.mean(u * n, axis=1, keepdims=True)
    gx_ref[...] = (gatt_ref[...].astype(f32) + root * (u - u_mean - n * un_mean)).astype(bf16)


def first_back(grad_qkv, weight, tokens, gatt, gain):
    rows, d = tokens.shape
    block = rows_of(ROW_BLOCK, d)
    return call(
        first_back_kernel,
        (rows // ROW_BLOCK,),
        [
            pl.BlockSpec((3, ROW_BLOCK, d), lambda i: (0, i, 0)),
            fixed((d, 3 * d)),
            block,
            block,
            fixed((1, d)),
        ],
        [block, kept((8, d))],
        [shape_of((rows, d), bf16), shape_of((8, d), f32)],
        micros=12,
        name="first_back",
    )(grad_qkv, weight, tokens, gatt, gain)


def dot_tn(a, b):
    return lax.dot_general(a, b, (((0,), (0,)), ((), ())), preferred_element_type=f32)


def expert_grad_kernel(
    up_owner_ref, down_owner_ref, arr_ref, gpre_ref, hidden_ref, garr_ref, up_ref, down_ref
):
    width = gpre_ref.shape[2]
    up = dot_tn(arr_ref[...], gpre_ref[0]).astype(bf16)
    for low in range(0, up.shape[0], width):
        up_ref[0, :, low : low + width] = up[low : low + width, :]
    down_ref[0] = dot_tn(hidden_ref[0], garr_ref[...]).astype(bf16)


def expert_grads(arriving, up_owners, down_owners, gpre, hidden, garr):
    _, rows, width = gpre.shape
    d = arriving.shape[1]
    m = up_owners.shape[0]
    return call(
        expert_grad_kernel,
        (m,),
        [
            fixed((rows, d)),
            pl.BlockSpec((1, rows, width), lambda t, up, down: (up[t], 0, 0)),
            pl.BlockSpec((1, rows, width), lambda t, up, down: (down[t], 0, 0)),
            fixed((rows, d)),
        ],
        [pl.BlockSpec((1, width, d), lambda t, *_: (t, 0, 0))] * 2,
        [shape_of((m, width, d), bf16)] * 2,
        prefetch=2,
        micros=7,
        name="expert_grads",
    )(up_owners, down_owners, arriving, gpre, hidden, garr)


def half_sums(terms):
    second = functools.reduce(lambda a, b: a + b, [ref[0].astype(f32) for ref in terms[1:]])
    return terms[0][0].astype(f32), second


def up_final_kernel(*refs):
    *terms, out_ref = refs
    width = terms[0].shape[2]
    for n, total in enumerate(half_sums(terms)):
        out_ref[:, n * width : (n + 1) * width] = total


def down_final_kernel(*refs):
    *terms, out_ref = refs
    for n, total in enumerate(half_sums(terms)):
        out_ref[n] = total


def up_final(*terms):
    _, width, d = terms[0].shape
    block = 128
    return call(
        up_final_kernel,
        (d // width, width // block),
        [pl.BlockSpec((1, block, width), lambda i, r: (0, r, i))] * len(terms),
        pl.BlockSpec((block, 2 * width), lambda i, r: (i * (width // block) + r, 0)),
        shape_of((d, 2 * width), f32),
        micros=7,
        name="up_final",
    )(*terms)


def down_final(*terms):
    _, width, d = terms[0].shape
    block = 128
    return call(
        down_final_kernel,
        (width // block,),
        [pl.BlockSpec((1, block, d), lambda r: (0, r, 0))] * len(terms),
        pl.BlockSpec((2, block, d), lambda r: (0, r, 0)),
        shape_of((2, width, d), f32),
        micros=7,
        name="down_final",
    )(*terms).reshape(2 * width, d)


def join_kernel(count, *refs):
    *terms, out_ref = refs
    left, right, lower = terms[:count], terms[count : 2 * count], terms[2 * count :]
    height, width = right[0].shape[2:]
    more = lower[0].shape[2]

    def total(parts):
        return functools.reduce(
            lambda a, b: a + b, [ref[0, 0].astype(f32) for ref in parts]
        ).astype(bf16)

    whole = total(left)
    out_ref[0, :height, :width] = whole[:height]
    out_ref[0, :height, width:] = total(right)
    out_ref[0, height : height + more, :] = total(lower)
    out_ref[0, height + more :, :width] = whole[height:]
    out_ref[0, height + more :, width:] = jnp.zeros_like(whole[height:])


def join(left, right, lower):
    levels, height, width = right.terms[0].shape[1:]
    more, rest = lower.terms[0].shape[2], left.terms[0].shape[2] - height
    if height % 16 or more % 16:
        left, right, lower = [part.finish(bf16) for part in (left, right, lower)]
        both = jnp.concatenate([left[:, :height], right], axis=2)
        last = jnp.pad(left[:, height:], ((0, 0), (0, 0), (0, width)))
        return jnp.concatenate([both, lower, last], axis=1)
    terms = left.terms + right.terms + lower.terms
    return Line.run(
        call(
            functools.partial(join_kernel, len(left.terms)),
            (levels,),
            [
                pl.BlockSpec((1, 1) + term.shape[2:], lambda z: (0, z, 0, 0)) for term in terms
            ],
            pl.BlockSpec((1, height + more + rest, 2 * width), lambda z: (z, 0, 0)),
            shape_of((levels, height + more + rest, 2 * width), bf16),
            micros=3,
            name="join",
        ),
        *terms,
    )


def swap(values, axis, bit):
    n = lax.axis_size(axis)
    return lax.ppermute(values, axis, [(i, i ^ bit) for i in range(n)])


def rows_kernel(sides, owner_ref, place_ref, ep_ref, a_ref, b_ref, *refs):
    *refs, grad_ref = refs
    extra_ref, out_refs = (refs[0], refs[1:]) if len(refs) % 2 else (None, refs)
    levels, height, width = out_refs[sides - 1].shape[1:]
    grad_ref[...] = dot_nn(a_ref[...], b_ref[...]).astype(bf16)
    for which in range(2):
        for z in range(levels):
            place = ep_ref[0] ^ (2 * reversed_bits(z, levels.bit_length() - 1) + 1 - which)
            rows = pl.ds(pl.multiple_of(place * height, height), height)
            for n in range(sides):
                out_refs[which * sides + n][0, z, :height, :] = grad_ref[
                    rows, n * width : (n + 1) * width
                ]
            if extra_ref is not None:
                out_refs[which * sides][0, z, height:, :] = extra_ref[0, place]


def rows_grad(a, b, owners, places, ep, copies, levels, sides, micros, extra=None):
    rows, d = b.shape
    height = a.shape[0] // (2 * copies * levels)
    width = d // sides
    if height % 16:
        away = [2 * reversed_bits(z, levels.bit_length() - 1) for z in range(levels)]

        def parts_of(values):
            values = jnp.take(values, owners, axis=0)
            return [
                jnp.take(values, ep[0] ^ (jnp.array(away, jnp.int32) + other), axis=1)
                for other in (1, 0)
            ]

        parts = parts_of(dot_nn(a, b).astype(bf16).reshape(copies, 2 * levels, height, d))
        result = [
            (part if n == 0 else jnp.take(part, places, axis=0))[
                ..., n * width : (n + 1) * width
            ]
            for part in parts
            for n in range(sides)
        ]
        if extra is not None:
            for which, rest in enumerate(parts_of(extra)):
                result[which * sides] = jnp.concatenate([result[which * sides], rest], axis=2)
        return result

    def shape(side):
        more = 0 if extra is None or side else extra.shape[2]
        return (levels, height + more, width)

    def piece(side):
        return pl.BlockSpec(
            (1,) + shape(side),
            lambda t, owner, place, ep: (place[t] if side else t, 0, 0, 0),
        )

    block = 2 * levels * height
    specs = [pl.BlockSpec((block, rows), lambda t, owner, *_: (owner[t], 0)), fixed((rows, d))]
    operands = [owners, places, ep, a, b]
    if extra is not None:
        specs.append(
            pl.BlockSpec((1,) + extra.shape[1:], lambda t, owner, *_: (owner[t], 0, 0, 0))
        )
        operands.append(extra)
    return call(
        functools.partial(rows_kernel, sides),
        (copies,),
        specs,
        [piece(side) for which in range(2) for side in range(sides)],
        [
            shape_of((copies,) + shape(side), bf16) for which in range(2) for side in range(sides)
        ],
        scratch=[pltpu.VMEM((block, d), bf16)],
        prefetch=3,
        micros=micros,
        name="rows_grad",
    )(*operands)


def add_kernel(*refs):
    *term_refs, out_ref = refs
    total = term_refs[0][...].astype(f32)
    for ref in term_refs[1:]:
        total = total + ref[...].astype(f32)
    out_ref[...] = total.astype(out_ref.dtype)


def add_terms(last, *others, first, count, kind):
    terms = [*others, last]
    shape = terms[0].shape
    columns = shape[-1]
    height = 1
    for extent in shape[1:-1]:
        height *= extent
    block = max(b for b in range(1, height + 1) if height % b == 0 and b * columns <= 1 << 18)
    result = call(
        add_kernel,
        (count, height // block),
        [pl.BlockSpec((1, block, columns), lambda t, r, *_: (first + t, r, 0)) for _ in terms],
        pl.BlockSpec((1, block, columns), lambda t, r, *_: (t, r, 0)),
        shape_of((count, height, columns), kind),
        micros=3,
        name="add_terms",
    )(*[term.reshape(term.shape[0], height, columns) for term in terms])
    return result.reshape((count,) + shape[1:])


class Halving:
    def __init__(self, terms, axis, bits, stride=1):
        self.terms, self.axis, self.bits, self.stride = terms, axis, list(bits), stride
        self.kind, self.extent = terms[0].dtype, 1 << len(self.bits)

    def add(self, first, kind):
        return Line.run(
            functools.partial(add_terms, first=first, count=self.extent, kind=kind),
            self.terms[-1], *self.terms[:-1],
        )

    def step(self, sent=None):
        if self.bits:
            if sent is None:
                self.extent //= 2
                sent = self.add(self.extent, self.kind)
            self.terms.append(swap(sent, self.axis, self.bits.pop(0) * self.stride))

    def finish(self, kind=f32):
        while self.bits:
            self.step()
        return self.add(0, kind)[0]


def reversed_bits(value, count):
    return sum(((value >> i) & 1) << (count - 1 - i) for i in range(count))


def shards(
    tokens, lengths, key_mask, routes, norm1_gain, norm1_bias, qkv_weight, out_weight,
    norm2_gain, norm2_bias, up_weight, down_weight, router_weight, mix_weight, expert_up,
    expert_down, cotangent,
):
    rows, d = tokens.shape
    groups, copies = lax.axis_size("ep"), lax.axis_size("dp")
    experts = expert_up.shape[0] * groups
    capacity = (5 * rows + 4 * experts - 1) // (4 * experts)
    slots = experts * capacity
    ep, dp = lax.axis_index("ep"), lax.axis_index("dp")
    core, level, levels = ep % 2, ep // 2, groups // 2
    count = copies.bit_length() - 1
    up_bits = [1 << i for i in reversed(range(count))]
    down_bits = [1 << i for i in range(count)]
    level_bits = [1 << i for i in range(levels.bit_length() - 1)]
    level_groups = [[2 * z + c for z in range(levels)] for c in range(2)]
    order = jnp.arange(copies, dtype=jnp.int32)
    back_order = jnp.array([reversed_bits(t, count) for t in range(copies)], jnp.int32)
    owners = dp.astype(jnp.int32) ^ order
    back_owners = dp.astype(jnp.int32) ^ back_order
    core_scalar = core.astype(jnp.int32).reshape(1)
    ep_scalar = ep.astype(jnp.int32).reshape(1)

    row_at = jnp.arange(rows, dtype=jnp.int32)
    live = row_at < lengths[0]
    flat_routes = routes[:, 0]
    routed = (flat_routes[:, None] == jnp.arange(experts)[None, :]) & live[:, None]
    ahead = dot_nn(
        (row_at[None, :] < row_at[:, None]).astype(bf16), routed.astype(bf16)
    )
    place = jnp.sum(jnp.where(routed, ahead, 0.0), axis=1).astype(jnp.int32)
    target = jnp.where(live, flat_routes * capacity + place, slots)
    target_column = target[:, None]
    pick = (jnp.arange(slots, dtype=jnp.int32)[:, None] == target[None, :]).astype(bf16)

    def exchange(values):
        return lax.all_to_all(
            values.reshape(groups, slots // groups, d), "ep", 0, 0, tiled=True
        ).reshape(slots, d)

    def sort_rows(values):
        return dot_nn(pick, values).astype(bf16)

    run = Line.run
    Line.last = None
    cot_arriving = exchange(run(sort_rows, cotangent))
    usable = live & (key_mask == 1)
    bias = jnp.where(usable, 0.0, MASKED).astype(f32)[:, None]
    mix_padded = jnp.pad(mix_weight, ((0, 0), (0, LANES - 2)))
    gate_padded = jnp.pad(
        jnp.concatenate([router_weight, mix_weight], axis=1),
        ((0, 0), (0, LANES - 2 - experts)),
    )
    first, qkv = run(ln_qkv, tokens, norm1_gain[None], norm1_bias[None], qkv_weight)
    context, context_t, lse = run(attend, qkv, bias)
    middle, second, second_t, gdl, gdl_t, mixing = run(
        after, tokens, core_scalar, context, cotangent, out_weight, norm2_gain[None],
        norm2_bias[None], mix_padded, d // groups,
    )
    cot_arriving, second = lax.optimization_barrier((cot_arriving, second))
    arriving = exchange(run(sort_rows, second))

    orders = (owners, up_bits), (back_owners, down_bits)
    parts = [
        run(dense, second, chunk, order, levels, second_t, gdl, gdl_t, up_weight, down_weight)
        for chunk, (order, _) in enumerate(orders)
    ]
    sums, lower = [], []
    half = copies // 2
    for (_, _, keep, send, keep_next, send_next), (_, bits) in zip(parts, orders):
        got_next, got = swap(send_next, "ep", 1), swap(send, "ep", 1)
        lower.append(got)
        sums.append(Halving([keep, got], "dp", bits))
        sums[-1].extent = half
        sums[-1].step(
            run(
                functools.partial(add_terms, first=0, count=half, kind=bf16), got_next, keep_next
            )
        )
    Line.others = tuple(lower)
    given = copies, ep_scalar, cot_arriving, gate_padded, expert_up[0], expert_down[0], experts
    m = copies // 2

    def expert_part(first, gpre, hidden):
        at = slice(m, None) if first else slice(0, m)
        return run(expert_grads, arriving, owners[at], back_owners[at], gpre, hidden, garr)

    def swapped(pair):
        return [swap(sent, "dp", bits[0]) for sent, bits in zip(pair, (up_bits, down_bits))]

    hidden0, gpre0, garr, *before = run(expert, arriving, 0, *given)
    got0 = swapped(expert_part(True, gpre0, hidden0))
    hidden1, gpre1, sent, gin, gate_grad = run(expert, arriving, 1, *given, [garr, *before])
    grad_back = exchange(gin)
    Line.others = tuple(side.terms[-1] for side in sums)
    dense_out, grad_second = run(
        dense_rest, parts[0][0], owners, back_order, parts[1][0], parts[0][1], parts[1][1], up_weight,
        down_weight,
    )
    got1 = swapped(expert_part(True, gpre1, hidden1))

    def halvings(keeps, gots):
        return [
            Halving([keep, got], "dp", bits[1:])
            for keep, got, bits in zip(keeps, gots, (up_bits, down_bits))
        ]

    halves0 = halvings(expert_part(False, gpre0, hidden0), got0)
    for side in halves0:
        side.step()
    halves1 = halvings(expert_part(False, gpre1, hidden1), got1)
    gatt, grad_context, sums2 = run(
        between, grad_second, target_column, grad_back, dense_out, middle, mixing, cotangent,
        second, mix_weight.T.astype(f32), norm2_gain[None], out_weight,
    )

    sent, gatt = lax.optimization_barrier((sent, gatt))
    expert_back = exchange(sent)

    def own_rows(a, b, all_bits, micros, extra=None):
        sides = len(all_bits)
        result = run(
            rows_grad, a, b, owners, back_order, ep_scalar, copies, levels, sides, micros,
            extra,
        )
        return [
            Halving([keep, swap(send, "ep", 1)], "dp", bits)
            for send, keep, bits in zip(result[:sides], result[sides:], all_bits)
        ]

    (out_side,) = own_rows(context_t, gatt, [up_bits], 3)
    grad_qkv, grad_qkv_t = run(attend_back, qkv, bias, lse, grad_context)
    done0 = [side.finish(bf16)[None] for side in halves0]
    for side in sums + halves1:
        side.step()
    grad_inputs, sums1 = run(first_back, grad_qkv, qkv_weight, tokens, gatt, norm1_gain[None])
    pieces = [
        lax.psum_scatter(
            side.finish(bf16).reshape(d, -1), "ep", scatter_dimension=0,
            axis_index_groups=level_groups, tiled=True,
        ).reshape(2, d // groups, -1)
        for side in sums
    ]
    home_mix = jnp.concatenate(
        [jnp.zeros((experts, d), f32), sums2[2:3], -sums2[2:3]], axis=0
    )
    small = jnp.concatenate(
        [sums1[:2], sums2[:2], gate_grad[: experts + 2] + home_mix], axis=0
    )
    kinds = small.shape[0]
    small = small.reshape(kinds, copies, groups, -1).transpose(1, 2, 0, 3)
    own = small.shape[3]
    small = small.reshape(copies, groups, 1, kinds * own).astype(bf16)
    small = jnp.pad(small, ((0, 0), (0, 0), (0, 15), (0, d // 2 - kinds * own)))
    qkv_sides = own_rows(
        grad_qkv_t.reshape(3 * d, rows), first, [up_bits, down_bits], 7, small
    )
    Line.others = tuple(side.terms[-1] for side in halves1)
    outputs = run(outputs_of, dense_out, target_column, expert_back, middle, mixing)
    for side in qkv_sides:
        side.step()
    out_side.step()
    expert_up_sum, expert_down_sum = [
        run(final, first_half, *second_half.terms)
        for final, first_half, second_half in zip((up_final, down_final), done0, halves1)
    ]
    for side in qkv_sides:
        side.step()
    out_side.step()
    whole = Halving([join(*qkv_sides, out_side)], "ep", level_bits, 2).finish()
    height = 3 * d // (copies * groups)
    qkv_sum, out_sum = whole[:height].T, whole[height : height + own]
    small = whole[height + own, : kinds * own].reshape(kinds, own).T
    pieces = [piece.astype(f32) for piece in pieces]
    up_sum, down_sum = [jnp.concatenate([piece[n] for piece in pieces], axis=1) for n in range(2)]
    down_sum = down_sum.T
    Line.last = None
    return (
        outputs, grad_inputs, small[:, 0], small[:, 1], qkv_sum, out_sum, small[:, 2],
        small[:, 3], up_sum, down_sum, small[:, 4 : 4 + experts], small[:, 4 + experts :],
        expert_up_sum[None], expert_down_sum[None],
    )


def solution(mesh):
    split = ("dp", "ep")
    return jax.shard_map(
        shards,
        mesh=mesh,
        in_specs=(
            P(split, None), P(split), P(split), P(split, None), P(), P(), P(), P(), P(), P(),
            P(), P(), P(), P(), P("ep", None, None), P("ep", None, None), P(split, None),
        ),
        out_specs=(
            P(split, None), P(split, None), P(split), P(split), P(None, split), P(split, None),
            P(split), P(split), P("ep", "dp"), P("dp", "ep"), P(split, None), P(split, None),
            P("ep", None, "dp"), P("ep", "dp", None),
        ),
        check_vma=False,
    )
```

```python
import functools

import jax
import jax.numpy as jnp
from jax import lax
from jax.experimental import pallas as pl
from jax.experimental.pallas import tpu as pltpu
from jax.sharding import PartitionSpec as P

HEAD_DIM = 64
EPSILON = 1e-05
MASKED = -1e30
ROW_BLOCK = 256
CHUNKS = 2
WEIGHT = 0.01
EXPERT_PARTS = 1
DENSE_BLOCK = 256
LANES = 128
GELU_ROOT = 0.7978845608028654
GELU_CUBE = 0.044715
LOG2_E = 1.4426950408889634

f32 = jnp.float32
bf16 = jnp.bfloat16


def dot_nn(a, b):
    return lax.dot_general(a, b, (((1,), (0,)), ((), ())), preferred_element_type=f32)


def dot_nt(a, b):
    return lax.dot_general(a, b, (((1,), (1,)), ((), ())), preferred_element_type=f32)


class Line:
    last = None
    others = ()

    @classmethod
    def run(cls, function, *values):
        result = function(*values)
        cls.last = jax.tree.leaves(result)[0]
        return result


def call(kernel, grid, in_specs, out_specs, out_shape, micros, scratch=(), prefetch=0, name=None):
    def apply(*operands):
        specs, count, ordered = list(in_specs), len(operands), kernel
        if Line.last is not None:
            unread = (Line.last,) + Line.others
            Line.others = ()
            specs += [pl.BlockSpec(memory_space=pl.ANY)] * len(unread)
            operands += unread

            def ordered(*refs):
                kernel(*refs[:count], *refs[count + len(unread) :])

        return pl.pallas_call(
            ordered,
            grid_spec=pltpu.PrefetchScalarGridSpec(
                num_scalar_prefetch=prefetch,
                grid=grid,
                in_specs=specs,
                out_specs=out_specs,
                scratch_shapes=list(scratch),
            ),
            out_shape=out_shape,
            compiler_params=pltpu.CompilerParams(
                dimension_semantics=("arbitrary",) * len(grid), vmem_limit_bytes=63 * 1024 * 1024
            ),
            cost_estimate=pl.CostEstimate(
                flops=int(micros * WEIGHT * 1.15e9),
                bytes_accessed=int(micros * WEIGHT * 3e6),
                transcendentals=0,
            ),
            name=name,
        )(*operands)

    return apply


def fixed(shape):
    return pl.BlockSpec(
        shape, lambda *_: (0,) * len(shape), pipeline_mode=pl.Buffered(buffer_count=1)
    )


def kept(shape):
    return pl.BlockSpec(shape, lambda *_: (0,) * len(shape))


def rows_of(height, width):
    return pl.BlockSpec((height, width), lambda i, *_: (i, 0))


def shape_of(shape, dtype):
    return jax.ShapeDtypeStruct(shape, dtype)


def normalized(values):
    average = jnp.mean(values, axis=1, keepdims=True)
    centered = values - average
    root = lax.rsqrt(jnp.mean(centered * centered, axis=1, keepdims=True) + EPSILON)
    return centered * root, root


def gelu_pair(v):
    square = v * v
    t = jnp.tanh(v * (GELU_ROOT + (GELU_ROOT * GELU_CUBE) * square))
    half = 0.5 + 0.5 * t
    slope = half + (v * (0.5 - 0.5 * (t * t))) * (
        GELU_ROOT + (3.0 * GELU_ROOT * GELU_CUBE) * square
    )
    return v * half, slope


def ln_qkv_kernel(x_ref, g_ref, b_ref, w_ref, first_ref, qkv_ref):
    @pl.when(pl.program_id(0) == 0)
    def _():
        def some_rows(i, carry):
            at = pl.ds(pl.multiple_of(i * LANES, LANES), LANES)
            n, _ = normalized(x_ref[at, :].astype(f32))
            first_ref[at, :] = (n * g_ref[...] + b_ref[...]).astype(bf16)
            return carry

        lax.fori_loop(0, x_ref.shape[0] // LANES, some_rows, 0)

    qkv_ref[...] = dot_nn(first_ref[...], w_ref[...]).astype(bf16)


def ln_qkv(tokens, gain, bias, weight):
    rows, d = tokens.shape
    width = weight.shape[1]
    block = 1024
    return call(
        ln_qkv_kernel,
        (width // block,),
        [
            fixed((rows, d)),
            fixed((1, d)),
            fixed((1, d)),
            pl.BlockSpec((d, block), lambda i: (0, i)),
        ],
        [kept((rows, d)), pl.BlockSpec((rows, block), lambda i: (0, i))],
        [shape_of((rows, d), bf16), shape_of((rows, width), bf16)],
        micros=11,
        name="ln_qkv",
    )(tokens, gain, bias, weight)


def diagonal_bias(bias_rows):
    size = bias_rows.shape[0]
    key_at = lax.broadcasted_iota(jnp.int32, (size, size), 0)
    query_at = lax.broadcasted_iota(jnp.int32, (size, size), 1)
    return jnp.where(
        key_at == query_at, 0.0, jnp.where(key_at < query_at, bias_rows, MASKED)
    )


def head_lanes(values, head):
    lane = lax.broadcasted_iota(jnp.int32, values.shape, 1)
    inside = (lane >= head * HEAD_DIM) & (lane < (head + 1) * HEAD_DIM)
    return jnp.where(inside, values, jnp.zeros_like(values))


def attend_kernel(bias_ref, q_ref, k_ref, v_ref, ctx_ref, ctx_t_ref, lse_ref):
    rows = q_ref.shape[0]
    v_t = v_ref[...].T
    for i in range(rows // ROW_BLOCK):
        low, high = i * ROW_BLOCK, (i + 1) * ROW_BLOCK
        edge = diagonal_bias(bias_ref[low:high, :])
        q = (q_ref[low:high, :].astype(f32) * (HEAD_DIM**-0.5 * LOG2_E)).astype(bf16)
        sides = []
        for head in range(2):
            q_head = head_lanes(q, head)
            inner = dot_nt(k_ref[low:high, :], q_head) + edge
            top = jnp.max(inner, axis=0, keepdims=True)
            if i:
                outer = dot_nt(k_ref[:low, :], q_head) + bias_ref[:low, :]
                top = jnp.maximum(top, jnp.max(outer, axis=0, keepdims=True))
            inner = jnp.exp2(inner - top)
            total = jnp.sum(inner, axis=0, keepdims=True)
            v_head = v_t[head * HEAD_DIM : (head + 1) * HEAD_DIM, :]
            side = dot_nn(v_head[:, low:high], inner.astype(bf16))
            if i:
                outer = jnp.exp2(outer - top)
                total = total + jnp.sum(outer, axis=0, keepdims=True)
                side = side + dot_nn(v_head[:, :low], outer.astype(bf16))
            sides.append(side / total)
            lse_ref[0, head : head + 1, low:high] = top + jnp.log2(total)
        both = jnp.concatenate(sides, axis=0)
        ctx_t_ref[:, low:high] = both.astype(bf16)
        ctx_ref[low:high, :] = both.T.astype(bf16)


def attend(qkv, bias):
    rows, d = qkv.shape[0], qkv.shape[1] // 3
    pairs = d // LANES

    def third(n):
        return pl.BlockSpec((rows, LANES), lambda h: (0, n * pairs + h))

    return call(
        attend_kernel,
        (pairs,),
        [fixed((rows, 1)), third(0), third(1), third(2)],
        [
            third(0),
            pl.BlockSpec((LANES, rows), lambda h: (h, 0)),
            pl.BlockSpec((1, 8, rows), lambda h: (h, 0, 0)),
        ],
        [
            shape_of((rows, d), bf16),
            shape_of((d, rows), bf16),
            shape_of((pairs, 8, rows), f32),
        ],
        micros=22,
        name="attend",
    )(bias, qkv, qkv, qkv)


def attend_back_kernel(
    bias_ref, lse_ref, q_ref, k_ref, v_ref, do_ref, g_ref, g_t_ref, gk_acc, gv_acc
):
    rows = q_ref.shape[0]
    scale = HEAD_DIM**-0.5
    k_t = k_ref[...].T
    gk_acc[...] = jnp.zeros_like(gk_acc)
    gv_acc[...] = jnp.zeros_like(gv_acc)
    for i in range(rows // ROW_BLOCK):
        low, high = i * ROW_BLOCK, (i + 1) * ROW_BLOCK
        edge = diagonal_bias(bias_ref[low:high, :])
        q = q_ref[low:high, :] * jnp.asarray(scale, bf16)
        raised = (q_ref[low:high, :].astype(f32) * (scale * LOG2_E)).astype(bf16)
        do = do_ref[low:high, :]
        sides = []
        for head in range(2):
            q_head = head_lanes(q, head)
            raised_head = head_lanes(raised, head)
            do_head = head_lanes(do, head)
            lse = lse_ref[0, head : head + 1, low:high]
            spans = [(low, high, edge)]
            if i:
                spans.append((0, low, bias_ref[:low, :]))
            probs, grads = [], []
            dots = 0.0
            for start, stop, bias in spans:
                p = jnp.exp2(dot_nt(k_ref[start:stop, :], raised_head) + bias - lse)
                gp = dot_nt(v_ref[start:stop, :], do_head)
                dots = dots + jnp.sum(p * gp, axis=0, keepdims=True)
                probs.append(p)
                grads.append(gp)
            side = 0.0
            k_head = k_t[head * HEAD_DIM : (head + 1) * HEAD_DIM, :]
            for (start, stop, _), p, gp in zip(spans, probs, grads):
                ds = (p * (gp - dots)).astype(bf16)
                gv_acc[start:stop, :] += dot_nn(p.astype(bf16), do_head)
                gk_acc[start:stop, :] += dot_nn(ds, q_head)
                side = side + dot_nn(k_head[:, start:stop], ds)
            sides.append(side * scale)
        both = jnp.concatenate(sides, axis=0)
        g_t_ref[0, :, low:high] = both.astype(bf16)
        g_ref[0, low:high, :] = both.T.astype(bf16)
    for n, acc in ((1, gk_acc), (2, gv_acc)):
        g_ref[n] = acc[...].astype(bf16)
        g_t_ref[n] = acc[...].T.astype(bf16)


def attend_back(qkv, bias, lse, grad_context):
    rows, d = grad_context.shape
    pairs = d // LANES

    def third(n):
        return pl.BlockSpec((rows, LANES), lambda h: (0, n * pairs + h))

    return call(
        attend_back_kernel,
        (pairs,),
        [
            fixed((rows, 1)),
            pl.BlockSpec((1, 8, rows), lambda h: (h, 0, 0)),
            third(0),
            third(1),
            third(2),
            third(0),
        ],
        [
            pl.BlockSpec((3, rows, LANES), lambda h: (0, 0, h)),
            pl.BlockSpec((3, LANES, rows), lambda h: (0, h, 0)),
        ],
        [shape_of((3, rows, d), bf16), shape_of((3, d, rows), bf16)],
        scratch=[pltpu.VMEM((rows, LANES), f32), pltpu.VMEM((rows, LANES), f32)],
        micros=28,
        name="attend_back",
    )(bias, lse, qkv, qkv, qkv, grad_context)


def after_kernel(
    rb, core_ref, x_ref, ctx_ref, cot_ref, w_ref, g_ref, b_ref, mix_ref,
    middle_ref, second_ref, second_t_ref, gdl_ref, gdl_t_ref, mixing_ref,
):
    d = x_ref.shape[1]
    middle = x_ref[...].astype(f32) + dot_nn(ctx_ref[...], w_ref[...])
    middle_ref[...] = middle
    n, _ = normalized(middle)
    second = (n * g_ref[...] + b_ref[...]).astype(bf16)
    second_ref[...] = second
    logits = dot_nn(second, mix_ref[...])
    gap = logits[:, 1:2] - logits[:, 0:1]
    first_share = 1.0 / (1.0 + jnp.exp(gap))
    other_share = 1.0 / (1.0 + jnp.exp(-gap))
    lane = lax.broadcasted_iota(jnp.int32, mixing_ref.shape, 1)
    mixing_ref[...] = jnp.where(lane == 0, first_share, other_share)
    gdl = (first_share * cot_ref[...].astype(f32)).astype(bf16)
    gdl_ref[...] = gdl
    core = core_ref[0]
    for values, target in ((second, second_t_ref), (gdl, gdl_t_ref)):
        turned = values.astype(f32).T.astype(bf16)
        for piece in range(d // rb):
            place = ((piece % 2) ^ core) * (d // (2 * rb)) + piece // 2
            target[pl.ds(pl.multiple_of(place * rb, rb), rb), :] = turned[
                piece * rb : (piece + 1) * rb, :
            ]


def after(tokens, core, context, cotangent, weight, gain, bias, mix_padded, rb):
    rows, d = tokens.shape
    block = rows_of(ROW_BLOCK, d)
    turned = pl.BlockSpec((d, ROW_BLOCK), lambda i, *_: (0, i))
    return call(
        functools.partial(after_kernel, rb),
        (rows // ROW_BLOCK,),
        [block, block, block, fixed((d, d)), fixed((1, d)), fixed((1, d)), fixed((d, LANES))],
        [block, block, turned, block, turned, rows_of(ROW_BLOCK, LANES)],
        [
            shape_of((rows, d), f32),
            shape_of((rows, d), bf16),
            shape_of((d, rows), bf16),
            shape_of((rows, d), bf16),
            shape_of((d, rows), bf16),
            shape_of((rows, LANES), f32),
        ],
        prefetch=1,
        micros=10,
        name="after",
    )(core, tokens, context, cotangent, weight, gain, bias, mix_padded)


def dense_kernel(
    owner_ref, second_ref, second_t_ref, gdl_ref, gdl_t_ref, up_ref, down_ref,
    hidden_ref, gpre_ref, keep_ref, send_ref, keep_next_ref, send_next_ref,
):
    rows = second_ref.shape[0]
    half = second_t_ref.shape[0] // 2
    levels = keep_ref.shape[1]
    for low in range(0, rows, DENSE_BLOCK):
        at = slice(low, low + DENSE_BLOCK)
        value, slope = gelu_pair(dot_nn(second_ref[at, :], up_ref[...]))
        hidden_ref[0, at, :] = value.astype(bf16)
        gpre_ref[0, at, :] = (dot_nt(gdl_ref[at, :], down_ref[...]) * slope).astype(bf16)

    def write(keep, send):
        for n, lhs_ref, units_ref in ((0, second_t_ref, gpre_ref), (1, gdl_t_ref, hidden_ref)):
            for target, low in ((keep, 0), (send, half)):
                grad = dot_nn(lhs_ref[low : low + half, :], units_ref[0]).astype(bf16)
                for z in range(levels):
                    target[0, z, n] = grad[z * (half // levels) : (z + 1) * (half // levels)]

    upper = pl.program_id(0) >= pl.num_programs(0) // 2
    pl.when(jnp.logical_not(upper))(lambda: write(keep_ref, send_ref))
    pl.when(upper)(lambda: write(keep_next_ref, send_next_ref))


def dense(second, chunk, owners, levels, second_t, gdl, gdl_t, up, down):
    rows, d = second.shape
    n = owners.shape[0]
    width = up.shape[1] // (n * CHUNKS)
    shape = (levels, 2, d // (2 * levels), width)
    lower = pl.BlockSpec((1,) + shape, lambda t, _: (jnp.minimum(t, n // 2 - 1), 0, 0, 0, 0))
    upper = pl.BlockSpec((1,) + shape, lambda t, _: (jnp.maximum(t - n // 2, 0), 0, 0, 0, 0))
    units = pl.BlockSpec((1, rows, width), lambda t, _: (t, 0, 0))
    return call(
        dense_kernel,
        (n,),
        [
            fixed((rows, d)),
            fixed((d, rows)),
            fixed((rows, d)),
            fixed((d, rows)),
            pl.BlockSpec((d, width), lambda t, owner: (0, owner[t] * CHUNKS + chunk)),
            pl.BlockSpec((width, d), lambda t, owner: (owner[t] * CHUNKS + chunk, 0)),
        ],
        [units, units, lower, lower, upper, upper],
        [shape_of((n, rows, width), bf16)] * 2
        + [shape_of((n // 2,) + shape, bf16)] * 4,
        prefetch=1,
        micros=100,
        name="dense",
    )(owners, second, second_t, gdl, gdl_t, up, down)


def dense_rest_kernel(
    owner_ref, place_ref, hidden0_ref, hidden1_ref, gpre0_ref, gpre1_ref, up_ref, down_ref,
    out_ref, gsec_ref,
):
    width = hidden0_ref.shape[2]

    @pl.when(pl.program_id(0) == 0)
    def _():
        out_ref[...] = jnp.zeros_like(out_ref)
        gsec_ref[...] = jnp.zeros_like(gsec_ref)

    out_ref[...] += dot_nn(hidden0_ref[0], down_ref[:width, :]) + dot_nn(
        hidden1_ref[0], down_ref[width:, :]
    )
    gsec_ref[...] += dot_nt(gpre0_ref[0], up_ref[:, :width]) + dot_nt(
        gpre1_ref[0], up_ref[:, width:]
    )


def dense_rest(hidden0, owners, places, hidden1, gpre0, gpre1, up, down):
    n, rows, width = hidden0.shape
    d = up.shape[0]
    units0 = pl.BlockSpec((1, rows, width), lambda t, owner, place: (t, 0, 0))
    units1 = pl.BlockSpec((1, rows, width), lambda t, owner, place: (place[t], 0, 0))
    return call(
        dense_rest_kernel,
        (n,),
        [
            units0,
            units1,
            units0,
            units1,
            pl.BlockSpec((d, 2 * width), lambda t, owner, _: (0, owner[t])),
            pl.BlockSpec((2 * width, d), lambda t, owner, _: (owner[t], 0)),
        ],
        [kept((rows, d))] * 2,
        [shape_of((rows, d), f32)] * 2,
        prefetch=2,
        micros=3000,
        name="dense_rest",
    )(owners, places, hidden0, hidden1, gpre0, gpre1, up, down)


def shares(logits, experts, me):
    lane = lax.broadcasted_iota(jnp.int32, logits.shape, 1)

    def softmax(inside):
        held = jnp.where(inside, logits, MASKED)
        raised = jnp.where(inside, jnp.exp(held - jnp.max(held, axis=1, keepdims=True)), 0.0)
        return raised / jnp.sum(raised, axis=1, keepdims=True)

    def pick(values, at):
        return jnp.sum(jnp.where(lane == at, values, 0.0), axis=1, keepdims=True)

    gates = softmax(lane < experts)
    mixing = softmax((lane >= experts) & (lane < experts + 2))
    return gates, pick(gates, me), pick(mixing, experts), pick(mixing, experts + 1)


def expert_step(arr_ref, garr_ref, up_ref, down_ref, hidden_ref, gpre_ref, out_acc, gin_acc):
    rows = arr_ref.shape[0]
    step = rows // EXPERT_PARTS
    for low in range(0, rows, step):
        at = slice(low, low + step)
        value, slope = gelu_pair(dot_nn(arr_ref[at, :], up_ref[...]))
        h = value.astype(bf16)
        g = (dot_nt(garr_ref[at, :], down_ref[...]) * slope).astype(bf16)
        gpre_ref[0, at, :] = g
        out_acc[at, :] += dot_nn(h, down_ref[...])
        gin_acc[at, :] += dot_nt(g, up_ref[...])
        hidden_ref[0, at, :] = h


def expert_first_kernel(
    experts, me_ref, arr_ref, cot_ref, gate_ref, up_ref, down_ref,
    hidden_ref, gpre_ref, garr_ref, logit_ref, out_acc, gin_acc,
):
    rows = arr_ref.shape[0]
    step = rows // EXPERT_PARTS

    @pl.when(pl.program_id(0) == 0)
    def _():
        out_acc[...] = jnp.zeros_like(out_acc)
        gin_acc[...] = jnp.zeros_like(gin_acc)
        for low in range(0, rows, step):
            at = slice(low, low + step)
            logits = dot_nn(arr_ref[at, :], gate_ref[...])
            logit_ref[at, :] = logits
            _, chosen, _, mix1 = shares(logits, experts, me_ref[0])
            garr_ref[at, :] = ((chosen * mix1) * cot_ref[at, :].astype(f32)).astype(bf16)

    expert_step(arr_ref, garr_ref, up_ref, down_ref, hidden_ref, gpre_ref, out_acc, gin_acc)


def expert_second_kernel(
    experts, me_ref, arr_ref, cot_ref, gate_ref, up_ref, down_ref, garr_ref, logit_ref, out_ref,
    grad_ref, hidden_ref, gpre_ref, sent_ref, gin_ref, gate_grad_ref, out_acc, gin_acc,
):
    rows = arr_ref.shape[0]
    step = rows // EXPERT_PARTS
    me = me_ref[0]

    @pl.when(pl.program_id(0) == 0)
    def _():
        out_acc[...] = out_ref[...]
        gin_acc[...] = grad_ref[...]

    expert_step(arr_ref, garr_ref, up_ref, down_ref, hidden_ref, gpre_ref, out_acc, gin_acc)

    @pl.when(pl.program_id(0) == pl.num_programs(0) - 1)
    def _():
        gate_grad = 0.0
        lane = lax.broadcasted_iota(jnp.int32, (step, LANES), 1)
        for low in range(0, rows, step):
            at = slice(low, low + step)
            gates, chosen, mix0, mix1 = shares(logit_ref[at, :], experts, me)
            out = out_acc[at, :]
            sent_ref[at, :] = ((chosen * mix1) * out).astype(bf16)
            met = jnp.sum(cot_ref[at, :].astype(f32) * out, axis=1, keepdims=True)
            grad_chosen = mix1 * met
            swing = chosen * met * mix0 * mix1
            grad = gates * grad_chosen * (jnp.where(lane == me, 1.0, 0.0) - chosen)
            grad = grad + jnp.where(lane == experts + 1, swing, 0.0)
            grad = grad - jnp.where(lane == experts, swing, 0.0)
            low_grad = grad.astype(bf16)
            gin_ref[at, :] = (gin_acc[at, :] + dot_nt(low_grad, gate_ref[...])).astype(bf16)
            gate_grad = gate_grad + dot_nn(grad.T.astype(bf16), arr_ref[at, :])
        gate_grad_ref[...] = gate_grad


def expert(arriving, half, n, me, cot, gate_padded, up, down, experts, before=None):
    rows, d = arriving.shape
    width = up.shape[1] // (2 * n)
    units = pl.BlockSpec((1, rows, width), lambda t, *_: (t, 0, 0))
    specs = [
        fixed((rows, d)),
        fixed((rows, d)),
        fixed((d, LANES)),
        pl.BlockSpec((d, width), lambda t, *_: (0, 2 * t + half)),
        pl.BlockSpec((width, d), lambda t, *_: (2 * t + half, 0)),
    ]
    shapes = [shape_of((n, rows, width), bf16)] * 2
    if half == 0:
        return call(
            functools.partial(expert_first_kernel, experts),
            (n,),
            specs,
            [units, units] + [kept((rows, d)), kept((rows, LANES))] + [kept((rows, d))] * 2,
            shapes
            + [shape_of((rows, d), bf16), shape_of((rows, LANES), f32)]
            + [shape_of((rows, d), f32)] * 2,
            prefetch=1,
            micros=4800,
            name="expert_first",
        )(me, arriving, cot, gate_padded, up, down)
    return call(
        functools.partial(expert_second_kernel, experts),
        (n,),
        specs + [fixed((rows, d)), fixed((rows, LANES)), fixed((rows, d)), fixed((rows, d))],
        [units, units] + [kept((rows, d))] * 2 + [kept((LANES, d))],
        shapes + [shape_of((rows, d), bf16)] * 2 + [shape_of((LANES, d), f32)],
        scratch=[pltpu.VMEM((rows, d), f32), pltpu.VMEM((rows, d), f32)],
        prefetch=1,
        micros=100,
        name="expert_second",
    )(me, arriving, cot, gate_padded, up, down, *before)


def between_kernel(
    target_ref, gin_ref, gs_ref, do_ref, middle_ref, mixing_ref, cot_ref,
    second_ref, mix_t_ref, g_ref, w_ref, gatt_ref, gctx_ref, sums_ref,
):
    @pl.when(pl.program_id(0) == 0)
    def _():
        sums_ref[...] = jnp.zeros_like(sums_ref)

    slots = gin_ref.shape[0]
    lane = lax.broadcasted_iota(jnp.int32, (ROW_BLOCK, slots), 1)
    pick = jnp.where(target_ref[...] == lane, 1.0, 0.0).astype(bf16)
    grad = gs_ref[...] + dot_nn(pick, gin_ref[...])
    go = cot_ref[...].astype(f32)
    met = jnp.sum(go * do_ref[...], axis=1, keepdims=True)
    swing = met * mixing_ref[:, 0:1] * mixing_ref[:, 1:2]
    grad = grad + swing * (mix_t_ref[0:1, :] - mix_t_ref[1:2, :])
    n, root = normalized(middle_ref[...])
    sums_ref[0:1, :] += jnp.sum(grad * n, axis=0, keepdims=True)
    sums_ref[1:2, :] += jnp.sum(grad, axis=0, keepdims=True)
    sums_ref[2:3, :] += jnp.sum(second_ref[...].astype(f32) * swing, axis=0, keepdims=True)
    u = grad * g_ref[...]
    u_mean = jnp.mean(u, axis=1, keepdims=True)
    un_mean = jnp.mean(u * n, axis=1, keepdims=True)
    gatt = (go + root * (u - u_mean - n * un_mean)).astype(bf16)
    gatt_ref[...] = gatt
    gctx_ref[...] = dot_nt(gatt, w_ref[...]).astype(bf16)


def between(gs, target, gin, do, middle, mixing, cotangent, second, mix_t, gain, weight):
    rows, d = middle.shape
    slots = gin.shape[0]
    block = rows_of(ROW_BLOCK, d)
    return call(
        between_kernel,
        (rows // ROW_BLOCK,),
        [
            rows_of(ROW_BLOCK, 1), fixed((slots, d)), block, block, block,
            rows_of(ROW_BLOCK, LANES), block, block, fixed((2, d)), fixed((1, d)), fixed((d, d)),
        ],
        [block, block, kept((8, d))],
        [shape_of((rows, d), bf16), shape_of((rows, d), bf16), shape_of((8, d), f32)],
        micros=12,
        name="between",
    )(
        target, gin, gs, do, middle, mixing, cotangent, second, mix_t, gain,
        weight,
    )


def out_kernel(target_ref, back_ref, do_ref, middle_ref, mixing_ref, out_ref):
    slots = back_ref.shape[0]
    lane = lax.broadcasted_iota(jnp.int32, (ROW_BLOCK, slots), 1)
    pick = jnp.where(target_ref[...] == lane, 1.0, 0.0).astype(bf16)
    mixed = mixing_ref[:, 0:1] * do_ref[...] + dot_nn(pick, back_ref[...])
    out_ref[...] = (middle_ref[...] + mixed).astype(bf16)


def outputs_of(do, target, back, middle, mixing):
    rows, d = middle.shape
    slots = back.shape[0]
    block = rows_of(ROW_BLOCK, d)
    return call(
        out_kernel,
        (rows // ROW_BLOCK,),
        [
            rows_of(ROW_BLOCK, 1), fixed((slots, d)), block, block,
            rows_of(ROW_BLOCK, LANES),
        ],
        block,
        shape_of((rows, d), bf16),
        micros=1000,
        name="outputs",
    )(target, back, do, middle, mixing)


def first_back_kernel(g_ref, w_ref, x_ref, gatt_ref, gain_ref, gx_ref, sums_ref):
    d = x_ref.shape[1]

    @pl.when(pl.program_id(0) == 0)
    def _():
        sums_ref[...] = jnp.zeros_like(sums_ref)

    grad = dot_nt(g_ref[0], w_ref[:, :d])
    grad = grad + dot_nt(g_ref[1], w_ref[:, d : 2 * d])
    grad = grad + dot_nt(g_ref[2], w_ref[:, 2 * d :])
    n, root = normalized(x_ref[...].astype(f32))
    sums_ref[0:1, :] += jnp.sum(grad * n, axis=0, keepdims=True)
    sums_ref[1:2, :] += jnp.sum(grad, axis=0, keepdims=True)
    u = grad * gain_ref[...]
    u_mean = jnp.mean(u, axis=1, keepdims=True)
    un_mean = jnp.mean(u * n, axis=1, keepdims=True)
    gx_ref[...] = (gatt_ref[...].astype(f32) + root * (u - u_mean - n * un_mean)).astype(bf16)


def first_back(grad_qkv, weight, tokens, gatt, gain):
    rows, d = tokens.shape
    block = rows_of(ROW_BLOCK, d)
    return call(
        first_back_kernel,
        (rows // ROW_BLOCK,),
        [
            pl.BlockSpec((3, ROW_BLOCK, d), lambda i: (0, i, 0)),
            fixed((d, 3 * d)),
            block,
            block,
            fixed((1, d)),
        ],
        [block, kept((8, d))],
        [shape_of((rows, d), bf16), shape_of((8, d), f32)],
        micros=12,
        name="first_back",
    )(grad_qkv, weight, tokens, gatt, gain)


def dot_tn(a, b):
    return lax.dot_general(a, b, (((0,), (0,)), ((), ())), preferred_element_type=f32)


def expert_grad_kernel(
    up_owner_ref, down_owner_ref, arr_ref, gpre_ref, hidden_ref, garr_ref, up_ref, down_ref
):
    width = gpre_ref.shape[2]
    up = dot_tn(arr_ref[...], gpre_ref[0]).astype(bf16)
    for low in range(0, up.shape[0], width):
        up_ref[0, :, low : low + width] = up[low : low + width, :]
    down_ref[0] = dot_tn(hidden_ref[0], garr_ref[...]).astype(bf16)


def expert_grads(arriving, up_owners, down_owners, gpre, hidden, garr):
    _, rows, width = gpre.shape
    d = arriving.shape[1]
    m = up_owners.shape[0]
    return call(
        expert_grad_kernel,
        (m,),
        [
            fixed((rows, d)),
            pl.BlockSpec((1, rows, width), lambda t, up, down: (up[t], 0, 0)),
            pl.BlockSpec((1, rows, width), lambda t, up, down: (down[t], 0, 0)),
            fixed((rows, d)),
        ],
        [pl.BlockSpec((1, width, d), lambda t, *_: (t, 0, 0))] * 2,
        [shape_of((m, width, d), bf16)] * 2,
        prefetch=2,
        micros=7,
        name="expert_grads",
    )(up_owners, down_owners, arriving, gpre, hidden, garr)


def half_sums(terms):
    second = functools.reduce(lambda a, b: a + b, [ref[0].astype(f32) for ref in terms[1:]])
    return terms[0][0].astype(f32), second


def up_final_kernel(*refs):
    *terms, out_ref = refs
    width = terms[0].shape[2]
    for n, total in enumerate(half_sums(terms)):
        out_ref[:, n * width : (n + 1) * width] = total


def down_final_kernel(*refs):
    *terms, out_ref = refs
    for n, total in enumerate(half_sums(terms)):
        out_ref[n] = total


def up_final(*terms):
    _, width, d = terms[0].shape
    block = 256
    return call(
        up_final_kernel,
        (d // width, width // block),
        [pl.BlockSpec((1, block, width), lambda i, r: (0, r, i))] * len(terms),
        pl.BlockSpec((block, 2 * width), lambda i, r: (i * (width // block) + r, 0)),
        shape_of((d, 2 * width), f32),
        micros=7,
        name="up_final",
    )(*terms)


def down_final(*terms):
    _, width, d = terms[0].shape
    block = 256
    return call(
        down_final_kernel,
        (width // block,),
        [pl.BlockSpec((1, block, d), lambda r: (0, r, 0))] * len(terms),
        pl.BlockSpec((2, block, d), lambda r: (0, r, 0)),
        shape_of((2, width, d), f32),
        micros=7,
        name="down_final",
    )(*terms).reshape(2 * width, d)


def join_kernel(count, *refs):
    *terms, out_ref = refs
    left, right, lower = terms[:count], terms[count : 2 * count], terms[2 * count :]
    height, width = right[0].shape[2:]
    more = lower[0].shape[2]

    def total(parts):
        return functools.reduce(
            lambda a, b: a + b, [ref[0, 0].astype(f32) for ref in parts]
        ).astype(bf16)

    whole = total(left)
    out_ref[0, :height, :width] = whole[:height]
    out_ref[0, :height, width:] = total(right)
    out_ref[0, height : height + more, :] = total(lower)
    out_ref[0, height + more :, :width] = whole[height:]
    out_ref[0, height + more :, width:] = jnp.zeros_like(whole[height:])


def join(left, right, lower):
    levels, height, width = right.terms[0].shape[1:]
    more, rest = lower.terms[0].shape[2], left.terms[0].shape[2] - height
    if height % 16 or more % 16:
        left, right, lower = [part.finish(bf16) for part in (left, right, lower)]
        both = jnp.concatenate([left[:, :height], right], axis=2)
        last = jnp.pad(left[:, height:], ((0, 0), (0, 0), (0, width)))
        return jnp.concatenate([both, lower, last], axis=1)
    terms = left.terms + right.terms + lower.terms
    return Line.run(
        call(
            functools.partial(join_kernel, len(left.terms)),
            (levels,),
            [
                pl.BlockSpec((1, 1) + term.shape[2:], lambda z: (0, z, 0, 0)) for term in terms
            ],
            pl.BlockSpec((1, height + more + rest, 2 * width), lambda z: (z, 0, 0)),
            shape_of((levels, height + more + rest, 2 * width), bf16),
            micros=3,
            name="join",
        ),
        *terms,
    )


def swap(values, axis, bit):
    n = lax.axis_size(axis)
    return lax.ppermute(values, axis, [(i, i ^ bit) for i in range(n)])


def rows_kernel(sides, owner_ref, place_ref, ep_ref, a_ref, b_ref, *refs):
    *refs, grad_ref = refs
    extra_ref, out_refs = (refs[0], refs[1:]) if len(refs) % 2 else (None, refs)
    levels, height, width = out_refs[sides - 1].shape[1:]
    grad_ref[...] = dot_nn(a_ref[...], b_ref[...]).astype(bf16)
    for which in range(2):
        for z in range(levels):
            place = ep_ref[0] ^ (2 * reversed_bits(z, levels.bit_length() - 1) + 1 - which)
            rows = pl.ds(pl.multiple_of(place * height, height), height)
            for n in range(sides):
                out_refs[which * sides + n][0, z, :height, :] = grad_ref[
                    rows, n * width : (n + 1) * width
                ]
            if extra_ref is not None:
                out_refs[which * sides][0, z, height:, :] = extra_ref[0, place]


def rows_grad(a, b, owners, places, ep, copies, levels, sides, micros, extra=None):
    rows, d = b.shape
    height = a.shape[0] // (2 * copies * levels)
    width = d // sides
    if height % 16:
        away = [2 * reversed_bits(z, levels.bit_length() - 1) for z in range(levels)]

        def parts_of(values):
            values = jnp.take(values, owners, axis=0)
            return [
                jnp.take(values, ep[0] ^ (jnp.array(away, jnp.int32) + other), axis=1)
                for other in (1, 0)
            ]

        parts = parts_of(dot_nn(a, b).astype(bf16).reshape(copies, 2 * levels, height, d))
        result = [
            (part if n == 0 else jnp.take(part, places, axis=0))[
                ..., n * width : (n + 1) * width
            ]
            for part in parts
            for n in range(sides)
        ]
        if extra is not None:
            for which, rest in enumerate(parts_of(extra)):
                result[which * sides] = jnp.concatenate([result[which * sides], rest], axis=2)
        return result

    def shape(side):
        more = 0 if extra is None or side else extra.shape[2]
        return (levels, height + more, width)

    def piece(side):
        return pl.BlockSpec(
            (1,) + shape(side),
            lambda t, owner, place, ep: (place[t] if side else t, 0, 0, 0),
        )

    block = 2 * levels * height
    specs = [pl.BlockSpec((block, rows), lambda t, owner, *_: (owner[t], 0)), fixed((rows, d))]
    operands = [owners, places, ep, a, b]
    if extra is not None:
        specs.append(
            pl.BlockSpec((1,) + extra.shape[1:], lambda t, owner, *_: (owner[t], 0, 0, 0))
        )
        operands.append(extra)
    return call(
        functools.partial(rows_kernel, sides),
        (copies,),
        specs,
        [piece(side) for which in range(2) for side in range(sides)],
        [
            shape_of((copies,) + shape(side), bf16) for which in range(2) for side in range(sides)
        ],
        scratch=[pltpu.VMEM((block, d), bf16)],
        prefetch=3,
        micros=micros,
        name="rows_grad",
    )(*operands)


def add_kernel(*refs):
    *term_refs, out_ref = refs
    total = term_refs[0][...].astype(f32)
    for ref in term_refs[1:]:
        total = total + ref[...].astype(f32)
    out_ref[...] = total.astype(out_ref.dtype)


def add_terms(last, *others, first, count, kind):
    terms = [*others, last]
    shape = terms[0].shape
    columns = shape[-1]
    height = 1
    for extent in shape[1:-1]:
        height *= extent
    block = max(b for b in range(1, height + 1) if height % b == 0 and b * columns <= 1 << 19)
    result = call(
        add_kernel,
        (count, height // block),
        [pl.BlockSpec((1, block, columns), lambda t, r, *_: (first + t, r, 0)) for _ in terms],
        pl.BlockSpec((1, block, columns), lambda t, r, *_: (t, r, 0)),
        shape_of((count, height, columns), kind),
        micros=3,
        name="add_terms",
    )(*[term.reshape(term.shape[0], height, columns) for term in terms])
    return result.reshape((count,) + shape[1:])


class Halving:
    def __init__(self, terms, axis, bits, stride=1):
        self.terms, self.axis, self.bits, self.stride = terms, axis, list(bits), stride
        self.kind, self.extent = terms[0].dtype, 1 << len(self.bits)

    def add(self, first, kind):
        return Line.run(
            functools.partial(add_terms, first=first, count=self.extent, kind=kind),
            self.terms[-1], *self.terms[:-1],
        )

    def step(self, sent=None):
        if self.bits:
            if sent is None:
                self.extent //= 2
                sent = self.add(self.extent, self.kind)
            self.terms.append(swap(sent, self.axis, self.bits.pop(0) * self.stride))

    def finish(self, kind=f32):
        while self.bits:
            self.step()
        return self.add(0, kind)[0]


def reversed_bits(value, count):
    return sum(((value >> i) & 1) << (count - 1 - i) for i in range(count))


def shards(
    tokens, lengths, key_mask, routes, norm1_gain, norm1_bias, qkv_weight, out_weight,
    norm2_gain, norm2_bias, up_weight, down_weight, router_weight, mix_weight, expert_up,
    expert_down, cotangent,
):
    rows, d = tokens.shape
    groups, copies = lax.axis_size("ep"), lax.axis_size("dp")
    experts = expert_up.shape[0] * groups
    capacity = (5 * rows + 4 * experts - 1) // (4 * experts)
    slots = experts * capacity
    ep, dp = lax.axis_index("ep"), lax.axis_index("dp")
    core, level, levels = ep % 2, ep // 2, groups // 2
    count = copies.bit_length() - 1
    up_bits = [1 << i for i in reversed(range(count))]
    down_bits = [1 << i for i in range(count)]
    level_bits = [1 << i for i in range(levels.bit_length() - 1)]
    level_groups = [[2 * z + c for z in range(levels)] for c in range(2)]
    order = jnp.arange(copies, dtype=jnp.int32)
    back_order = jnp.array([reversed_bits(t, count) for t in range(copies)], jnp.int32)
    owners = dp.astype(jnp.int32) ^ order
    back_owners = dp.astype(jnp.int32) ^ back_order
    core_scalar = core.astype(jnp.int32).reshape(1)
    ep_scalar = ep.astype(jnp.int32).reshape(1)

    row_at = jnp.arange(rows, dtype=jnp.int32)
    live = row_at < lengths[0]
    flat_routes = routes[:, 0]
    routed = (flat_routes[:, None] == jnp.arange(experts)[None, :]) & live[:, None]
    ahead = dot_nn(
        (row_at[None, :] < row_at[:, None]).astype(bf16), routed.astype(bf16)
    )
    place = jnp.sum(jnp.where(routed, ahead, 0.0), axis=1).astype(jnp.int32)
    target = jnp.where(live, flat_routes * capacity + place, slots)
    target_column = target[:, None]
    pick = (jnp.arange(slots, dtype=jnp.int32)[:, None] == target[None, :]).astype(bf16)

    def exchange(values):
        return lax.all_to_all(
            values.reshape(groups, slots // groups, d), "ep", 0, 0, tiled=True
        ).reshape(slots, d)

    def sort_rows(values):
        return dot_nn(pick, values).astype(bf16)

    run = Line.run
    Line.last = None
    cot_arriving = exchange(run(sort_rows, cotangent))
    usable = live & (key_mask == 1)
    bias = jnp.where(usable, 0.0, MASKED).astype(f32)[:, None]
    mix_padded = jnp.pad(mix_weight, ((0, 0), (0, LANES - 2)))
    gate_padded = jnp.pad(
        jnp.concatenate([router_weight, mix_weight], axis=1),
        ((0, 0), (0, LANES - 2 - experts)),
    )
    first, qkv = run(ln_qkv, tokens, norm1_gain[None], norm1_bias[None], qkv_weight)
    context, context_t, lse = run(attend, qkv, bias)
    middle, second, second_t, gdl, gdl_t, mixing = run(
        after, tokens, core_scalar, context, cotangent, out_weight, norm2_gain[None],
        norm2_bias[None], mix_padded, d // groups,
    )
    cot_arriving, second = lax.optimization_barrier((cot_arriving, second))
    arriving = exchange(run(sort_rows, second))

    orders = (owners, up_bits), (back_owners, down_bits)
    parts = [
        run(dense, second, chunk, order, levels, second_t, gdl, gdl_t, up_weight, down_weight)
        for chunk, (order, _) in enumerate(orders)
    ]
    sums, lower = [], []
    half = copies // 2
    for (_, _, keep, send, keep_next, send_next), (_, bits) in zip(parts, orders):
        got_next, got = swap(send_next, "ep", 1), swap(send, "ep", 1)
        lower.append(got)
        sums.append(Halving([keep, got], "dp", bits))
        sums[-1].extent = half
        sums[-1].step(
            run(
                functools.partial(add_terms, first=0, count=half, kind=bf16), got_next, keep_next
            )
        )
    Line.others = tuple(lower)
    given = copies, ep_scalar, cot_arriving, gate_padded, expert_up[0], expert_down[0], experts
    m = copies // 2

    def expert_part(first, gpre, hidden):
        at = slice(m, None) if first else slice(0, m)
        return run(expert_grads, arriving, owners[at], back_owners[at], gpre, hidden, garr)

    def swapped(pair):
        return [swap(sent, "dp", bits[0]) for sent, bits in zip(pair, (up_bits, down_bits))]

    hidden0, gpre0, garr, *before = run(expert, arriving, 0, *given)
    got0 = swapped(expert_part(True, gpre0, hidden0))
    hidden1, gpre1, sent, gin, gate_grad = run(expert, arriving, 1, *given, [garr, *before])
    grad_back = exchange(gin)
    Line.others = tuple(side.terms[-1] for side in sums)
    dense_out, grad_second = run(
        dense_rest, parts[0][0], owners, back_order, parts[1][0], parts[0][1], parts[1][1], up_weight,
        down_weight,
    )
    got1 = swapped(expert_part(True, gpre1, hidden1))

    def halvings(keeps, gots):
        return [
            Halving([keep, got], "dp", bits[1:])
            for keep, got, bits in zip(keeps, gots, (up_bits, down_bits))
        ]

    halves0 = halvings(expert_part(False, gpre0, hidden0), got0)
    for side in halves0:
        side.step()
    halves1 = halvings(expert_part(False, gpre1, hidden1), got1)
    gatt, grad_context, sums2 = run(
        between, grad_second, target_column, grad_back, dense_out, middle, mixing, cotangent,
        second, mix_weight.T.astype(f32), norm2_gain[None], out_weight,
    )

    sent, gatt = lax.optimization_barrier((sent, gatt))
    expert_back = exchange(sent)

    def own_rows(a, b, all_bits, micros, extra=None):
        sides = len(all_bits)
        result = run(
            rows_grad, a, b, owners, back_order, ep_scalar, copies, levels, sides, micros,
            extra,
        )
        return [
            Halving([keep, swap(send, "ep", 1)], "dp", bits)
            for send, keep, bits in zip(result[:sides], result[sides:], all_bits)
        ]

    (out_side,) = own_rows(context_t, gatt, [up_bits], 3)
    grad_qkv, grad_qkv_t = run(attend_back, qkv, bias, lse, grad_context)
    done0 = [side.finish(bf16)[None] for side in halves0]
    for side in sums + halves1:
        side.step()
    grad_inputs, sums1 = run(first_back, grad_qkv, qkv_weight, tokens, gatt, norm1_gain[None])
    pieces = [
        lax.psum_scatter(
            side.finish(bf16).reshape(d, -1), "ep", scatter_dimension=0,
            axis_index_groups=level_groups, tiled=True,
        ).reshape(2, d // groups, -1)
        for side in sums
    ]
    home_mix = jnp.concatenate(
        [jnp.zeros((experts, d), f32), sums2[2:3], -sums2[2:3]], axis=0
    )
    small = jnp.concatenate(
        [sums1[:2], sums2[:2], gate_grad[: experts + 2] + home_mix], axis=0
    )
    kinds = small.shape[0]
    small = small.reshape(kinds, copies, groups, -1).transpose(1, 2, 0, 3)
    own = small.shape[3]
    small = small.reshape(copies, groups, 1, kinds * own).astype(bf16)
    small = jnp.pad(small, ((0, 0), (0, 0), (0, 15), (0, d // 2 - kinds * own)))
    qkv_sides = own_rows(
        grad_qkv_t.reshape(3 * d, rows), first, [up_bits, down_bits], 7, small
    )
    Line.others = tuple(side.terms[-1] for side in halves1)
    outputs = run(outputs_of, dense_out, target_column, expert_back, middle, mixing)
    for side in qkv_sides:
        side.step()
    out_side.step()
    expert_up_sum, expert_down_sum = [
        run(final, first_half, *second_half.terms)
        for final, first_half, second_half in zip((up_final, down_final), done0, halves1)
    ]
    for side in qkv_sides:
        side.step()
    out_side.step()
    whole = Halving([join(*qkv_sides, out_side)], "ep", level_bits, 2).finish()
    height = 3 * d // (copies * groups)
    qkv_sum, out_sum = whole[:height].T, whole[height : height + own]
    small = whole[height + own, : kinds * own].reshape(kinds, own).T
    pieces = [piece.astype(f32) for piece in pieces]
    up_sum, down_sum = [jnp.concatenate([piece[n] for piece in pieces], axis=1) for n in range(2)]
    down_sum = down_sum.T
    Line.last = None
    return (
        outputs, grad_inputs, small[:, 0], small[:, 1], qkv_sum, out_sum, small[:, 2],
        small[:, 3], up_sum, down_sum, small[:, 4 : 4 + experts], small[:, 4 + experts :],
        expert_up_sum[None], expert_down_sum[None],
    )


def solution(mesh):
    split = ("dp", "ep")
    return jax.shard_map(
        shards,
        mesh=mesh,
        in_specs=(
            P(split, None), P(split), P(split), P(split, None), P(), P(), P(), P(), P(), P(),
            P(), P(), P(), P(), P("ep", None, None), P("ep", None, None), P(split, None),
        ),
        out_specs=(
            P(split, None), P(split, None), P(split), P(split), P(None, split), P(split, None),
            P(split), P(split), P("ep", "dp"), P("dp", "ep"), P(split, None), P(split, None),
            P("ep", None, "dp"), P("ep", "dp", None),
        ),
        check_vma=False,
    )
```
